128 devices in a mesh: row: 8 (over x, core), col: 16 (over y, z).
Axes of the slice: x: 4, y: 4, z: 4, core: 2. Of those that a mesh axis runs over, the one named last changes fastest.
Arguments:
- edge_h: int32 [256, 2048], P('row', 'col'), may hold values from 0 to 7
- edge_v: int32 [256, 2048], P('row', 'col'), may hold values from 0 to 7
- pads: int32 [256, 2048], P('row', 'col'), may hold values 0 or 1
- loads: int32 [256, 256, 2048], P(None, 'row', 'col'), may hold values from 0 to 7
- scales: float32 [256, 8], replicated, may hold values from 0.25 to 4
Outputs:
- drop: float32 [256, 256, 2048], P(None, 'row', 'col')
- res_norms: float32 [256, 5], replicated
The draws below stay inside these ranges and needn't reach their ends.
All inputs are finite; a program needn't handle non-finite values. No bound on the sum of `pads` on one device may be relied on, other than what follows from the above.
Results may differ from the reference program's by a relative error of at most 0.0003.
Values sent between devices are 32-bit elements; how exact they have to be, the bound alone decides.
No kernel may reach another device: no remote copies, remote signals or barrier semaphores. Data moves between devices by JAX's collectives and lax.ppermute only.
A program may use at most 128 MiB of HBM per device.

```python
import math
import jax
import jax.numpy as jnp
from jax import lax

SCEN = 256
ITERS = 4
NR = 256
NC = 2048


def plant(entries, key, least, high):
    shape = entries.shape
    spot = [jax.random.randint(jax.random.fold_in(key, axis), (), 0, shape[axis]) for axis in range(len(shape))]
    entries = entries.at[tuple(spot)].set(least)
    longest = shape.index(max(shape))
    spot[longest] = (spot[longest] + 1) % shape[longest]
    return entries.at[tuple(spot)].set(high)


def setup_inputs(seed: int = 0) -> dict:
    streams_of = jax.random.split(jax.random.key(seed), 6)
    edge_h = plant(jax.random.randint(streams_of[0], (NR, NC), 0, 8), jax.random.fold_in(streams_of[0], 1), 0, 7).astype(jnp.int32)
    edge_v = plant(jax.random.randint(streams_of[1], (NR, NC), 0, 8), jax.random.fold_in(streams_of[1], 1), 0, 7).astype(jnp.int32)
    pads = plant((jax.random.randint(streams_of[2], (NR, NC), 0, 16) < 1).astype(jnp.int32), jax.random.fold_in(streams_of[2], 1), 0, 1)
    loads = plant(jax.random.randint(streams_of[3], (SCEN, NR, NC), 0, 8), jax.random.fold_in(streams_of[3], 1), 0, 7).astype(jnp.int32)
    scales = jnp.clip(jnp.exp(jax.random.uniform(streams_of[4], (SCEN, 8), jnp.float32, math.log(0.25), math.log(4.0))), 0.25, 4.0)
    return dict(edge_h=edge_h, edge_v=edge_v, pads=pads, loads=loads, scales=scales)


edge_table = (0.5, 0.8, 1.2, 1.7, 2.3, 3.0, 3.8, 4.7)
load_table = (0.25, 0.5, 1.0, 1.5, 2.0, 3.0, 4.0, 6.0)
pad_conductance = 20.0
leakage = 0.05

def lookup(classes, table):
    total = jnp.zeros(classes.shape, jnp.float32)
    for number, amount in enumerate(table):
        total = total + jnp.where(classes == number, jnp.float32(amount), jnp.float32(0.0))
    return total

def apply_grid(field, g_east, g_west, g_south, g_north, diagonal):
    padded = jnp.pad(field, 1)
    north = padded[:-2, 1:-1]
    south = padded[2:, 1:-1]
    west = padded[1:-1, :-2]
    east = padded[1:-1, 2:]
    return diagonal * field - (g_east * east + g_west * west + g_south * south + g_north * north)

def reference(edge_h, edge_v, pads, loads, scales):
    rows_all, cols_all = pads.shape
    row_ids = lax.broadcasted_iota(jnp.int32, pads.shape, 0)
    col_ids = lax.broadcasted_iota(jnp.int32, pads.shape, 1)
    zero = jnp.zeros(pads.shape, jnp.float32)
    g_east = jnp.where(col_ids < cols_all - 1, lookup(edge_h, edge_table), zero)
    g_south = jnp.where(row_ids < rows_all - 1, lookup(edge_v, edge_table), zero)
    g_west = jnp.pad(g_east[:, :-1], ((0, 0), (1, 0)))
    g_north = jnp.pad(g_south[:-1], ((1, 0), (0, 0)))
    diagonal = g_east + g_west + g_south + g_north + pads.astype(jnp.float32) * pad_conductance + leakage
    weights = -scales.astype(jnp.float32) * jnp.asarray(load_table, jnp.float32)[None, :]

    def solve_one(pair):
        weight_row, load_map = pair
        right = jnp.zeros(load_map.shape, jnp.float32)
        for number in range(8):
            right = right + jnp.where(load_map == number, weight_row[number], jnp.float32(0.0))
        solution = jnp.zeros_like(right)
        resid = right
        precond = resid / diagonal
        direction = precond
        gamma = jnp.sum(resid * precond)
        norms = [jnp.sqrt(jnp.sum(resid * resid))]
        for iteration in range(ITERS):
            image = apply_grid(direction, g_east, g_west, g_south, g_north, diagonal)
            alpha = gamma / jnp.sum(direction * image)
            solution = solution + alpha * direction
            resid = resid - alpha * image
            precond = resid / diagonal
            gamma_new = jnp.sum(resid * precond)
            norms.append(jnp.sqrt(jnp.sum(resid * resid)))
            direction = precond + gamma_new / gamma * direction
            gamma = gamma_new
        return (solution, jnp.stack(norms))
    drop, res_norms = lax.map(solve_one, (weights, loads))
    return (drop, res_norms)
```

```python
import functools

import jax
import jax.numpy as jnp
from jax import lax
from jax.experimental import pallas as pl
from jax.experimental.pallas import tpu as pltpu
from jax.sharding import Mesh
from jax.sharding import PartitionSpec as P

ITERS = 4
ROW = ("x", "core")
COL = ("y", "z")

edge_table = (0.5, 0.8, 1.2, 1.7, 2.3, 3.0, 3.8, 4.7)
load_table = (0.25, 0.5, 1.0, 1.5, 2.0, 3.0, 4.0, 6.0)
pad_conductance = 20.0
leakage = 0.05

LANES = 128
TILE = 8
HALO = ITERS
SUMS = 24
MIB = 1024 * 1024


def lookup(classes, table):
    total = jnp.zeros(classes.shape, jnp.float32)
    for number, amount in enumerate(table):
        total = total + jnp.where(classes == number, jnp.float32(amount), jnp.float32(0.0))
    return total


def prepare_kernel(loads_ref, table_ref, classes_ref, rhs_ref, west_ref, east_ref):
    step = pl.program_id(0)
    scen, rows, cols = loads_ref.shape
    flat = loads_ref.reshape(scen * rows, cols)
    for row in range(rows):
        for half in range(scen // LANES):
            index = flat[pl.ds(half * LANES * rows + row, LANES, stride=rows), :]
            table = table_ref[half * LANES : (half + 1) * LANES, :]
            value = jnp.take_along_axis(table, index, axis=1)
            turned = value.T
            lanes = slice(half * LANES, (half + 1) * LANES)
            rhs_ref[row, :, lanes] = turned
            west_ref[step * rows + row, :, lanes] = turned[:TILE]
            east_ref[step * rows + row, :, lanes] = turned[cols - TILE :]

    @pl.when(step == 0)
    def _():
        first = rows * pl.num_programs(0)
        for tile in range(classes_ref.shape[0] // TILE):
            piece = classes_ref[tile * TILE : (tile + 1) * TILE, :]
            lanes = slice((tile % 2) * LANES, (tile % 2 + 1) * LANES)
            west_ref[first + tile // 2, :, lanes] = piece
            east_ref[first + tile // 2, :, lanes] = piece


def prepare(loads, table, classes):
    scen, rows, cols = loads.shape
    extra = classes.shape[0] // TILE // 2
    side = jax.ShapeDtypeStruct((rows + extra, TILE, scen), jnp.float32)
    return pl.pallas_call(
        prepare_kernel,
        grid=(rows // TILE,),
        in_specs=[
            pl.BlockSpec((scen, TILE, cols), lambda i: (0, i, 0)),
            pl.BlockSpec(table.shape, lambda i: (0, 0)),
            pl.BlockSpec(classes.shape, lambda i: (0, 0)),
        ],
        out_specs=[
            pl.BlockSpec((TILE, cols, scen), lambda i: (i, 0, 0)),
            pl.BlockSpec(side.shape, lambda i: (0, 0, 0)),
            pl.BlockSpec(side.shape, lambda i: (0, 0, 0)),
        ],
        out_shape=[jax.ShapeDtypeStruct((rows, cols, scen), jnp.float32), side, side],
        compiler_params=pltpu.CompilerParams(vmem_limit_bytes=24 * MIB),
    )(loads, table, classes)


def message_kernel(up_ref, down_ref, from_west, from_east, classes_ref, north_ref, south_ref):
    rows = classes_ref.shape[0] // 3
    cols = up_ref.shape[1]
    across = cols // TILE + 2

    def class_tile(ref, tile):
        return ref[rows + tile // 2, :, (tile % 2) * LANES : (tile % 2 + 1) * LANES]

    for out, own, top in ((north_ref, up_ref, 0), (south_ref, down_ref, rows - HALO)):
        for row in range(HALO):
            out[row * across] = from_west[top + row]
            out[row * across + 1 : row * across + across - 1] = own[row].reshape(
                across - 2, TILE, own.shape[2]
            )
            out[row * across + across - 1] = from_east[top + row]
        number = 0
        for array in range(3):
            tile = (array * rows + (top // TILE) * TILE) // TILE
            middle = classes_ref[tile * TILE : (tile + 1) * TILE, :]
            for piece in (class_tile(from_west, tile), middle, class_tile(from_east, tile)):
                lanes = slice((number % 2) * LANES, (number % 2 + 1) * LANES)
                out[HALO * across + number // 2, :, lanes] = piece
                number += 1
        out[HALO * across + number // 2, :, LANES:] = jnp.zeros((TILE, LANES), jnp.float32)


def messages(rhs, from_west, from_east, classes):
    rows, cols, scen = rhs.shape
    out = jax.ShapeDtypeStruct((HALO * (cols // TILE + 2) + 5, TILE, scen), jnp.float32)
    whole = lambda a: pl.BlockSpec(a.shape, lambda i, n=len(a.shape): (0,) * n)
    return pl.pallas_call(
        message_kernel,
        grid=(1,),
        in_specs=[
            pl.BlockSpec((HALO, cols, scen), lambda i: (0, 0, 0)),
            pl.BlockSpec((HALO, cols, scen), lambda i: (rows // HALO - 1, 0, 0)),
            whole(from_west),
            whole(from_east),
            whole(classes),
        ],
        out_specs=[whole(out), whole(out)],
        out_shape=[out, out],
        compiler_params=pltpu.CompilerParams(vmem_limit_bytes=16 * MIB),
    )(rhs, rhs, from_west, from_east, classes)


def basis_kernel(
    pos_ref, rhs_ref, west_ref, east_ref, north_ref, south_ref, classes_ref,
    v0_out, v1_out, v2_out, v3_out, sums_ref,
    small_ref, turned_ref, ge_ref, gs_ref, di_ref, dg_ref, v0, v1, v2, v3, sem,
):
    rows, cols, scen = rhs_ref.shape
    halves = scen // LANES
    across = cols // TILE + 2
    tall = rows + 2 * HALO
    first = 2 * TILE
    outs, fields = (v0_out, v1_out, v2_out, v3_out), (v0, v1, v2, v3)

    def side_class(ref, tile):
        return ref[rows + tile // 2, :, (tile % 2) * LANES : (tile % 2 + 1) * LANES]

    def end_class(ref, number):
        return ref[HALO * across + number // 2, :, (number % 2) * LANES : (number % 2 + 1) * LANES]

    for array in range(3):
        for part in range(3):
            lanes = slice(part * LANES, (part + 1) * LANES)
            small_ref[array, 0:TILE, lanes] = end_class(north_ref, array * 3 + part)
            small_ref[array, TILE + rows : 2 * TILE + rows, lanes] = end_class(south_ref, array * 3 + part)
            for tile in range(rows // TILE):
                number = array * (rows // TILE) + tile
                if part == 1:
                    piece = classes_ref[number * TILE : (number + 1) * TILE, :]
                else:
                    piece = side_class(west_ref if part == 0 else east_ref, number)
                small_ref[array, (tile + 1) * TILE : (tile + 2) * TILE, lanes] = piece
    shape = small_ref.shape[1:]
    row_ids = pos_ref[0] * rows - TILE + lax.broadcasted_iota(jnp.int32, shape, 0)
    col_ids = pos_ref[1] * cols - LANES + lax.broadcasted_iota(jnp.int32, shape, 1)
    row_ok = (row_ids >= 0) & (row_ids < pos_ref[2])
    col_ok = (col_ids >= 0) & (col_ids < pos_ref[3])
    zero = jnp.zeros(shape, jnp.float32)
    g_east = jnp.where(row_ok & col_ok & (col_ids < pos_ref[3] - 1), lookup(small_ref[0], edge_table), zero)
    g_south = jnp.where(row_ok & col_ok & (row_ids < pos_ref[2] - 1), lookup(small_ref[1], edge_table), zero)
    g_west = pltpu.roll(g_east, 1, 1)
    g_north = pltpu.roll(g_south, 1, 0)
    diagonal = g_east + g_west + g_south + g_north + small_ref[2] * pad_conductance + leakage
    for source, out in (
        (g_east, ge_ref), (g_south, gs_ref), (1.0 / diagonal, di_ref), (diagonal, dg_ref),
    ):
        padded = jnp.concatenate([source, jnp.zeros((LANES - shape[0], shape[1]), jnp.float32)], axis=0)
        for part in range(3):
            turned_ref[part * LANES : (part + 1) * LANES, :] = padded[:, part * LANES : (part + 1) * LANES].T

        def spread(tile, carry, out=out):
            start = pl.multiple_of(LANES - first + tile * TILE, TILE)
            piece = turned_ref[pl.ds(start, TILE), :]
            at = pl.multiple_of(tile * TILE, TILE)
            for row in range(tall):
                lane = TILE - HALO + row
                out[row, pl.ds(at, TILE), :] = jnp.broadcast_to(piece[:, lane : lane + 1], (TILE, LANES))
            return carry

        lax.fori_loop(0, cols // TILE + 4, spread, 0)

    def start_own(tile, carry):
        at = pl.multiple_of(tile * TILE, TILE)
        here = pl.multiple_of(first + tile * TILE, TILE)
        for row in range(rows):
            di = di_ref[row + HALO, pl.ds(here, TILE), :]
            for half in range(halves):
                lanes = slice(half * LANES, (half + 1) * LANES)
                v0[half, row + HALO, pl.ds(here, TILE), :] = rhs_ref[row, pl.ds(at, TILE), lanes] * di
        return carry

    lax.fori_loop(0, cols // TILE, start_own, 0)
    for half in range(halves):
        lanes = slice(half * LANES, (half + 1) * LANES)
        for row in range(rows):
            for ref, at in ((west_ref, TILE), (east_ref, first + cols)):
                v0[half, row + HALO, at : at + TILE, :] = (
                    ref[row, :, lanes] * di_ref[row + HALO, at : at + TILE, :]
                )
        for row in range(HALO):
            for ref, at in ((north_ref, row), (south_ref, HALO + rows + row)):
                block = ref[row * across : (row + 1) * across, :, lanes].reshape(across * TILE, LANES)
                v0[half, at, TILE : TILE + across * TILE, :] = block * di_ref[at, TILE : TILE + across * TILE, :]

    def copies(level):
        return [
            pltpu.make_async_copy(
                fields[level].at[half, HALO : HALO + rows, first : first + cols, :],
                outs[level].at[half],
                sem.at[level * halves + half],
            )
            for half in range(halves)
        ]

    for copy in copies(0):
        copy.start()
    for level in range(ITERS - 1):
        old, new = fields[level], fields[level + 1]
        top, bottom = level + 1, tall - level - 1

        def apply(tile, carry, old=old, new=new, top=top, bottom=bottom):
            at = tile * TILE
            here = pl.ds(pl.multiple_of(at, TILE), TILE)
            east, west = pl.ds(at + 1, TILE), pl.ds(at - 1, TILE)
            north = [old[half, top - 1, here, :] for half in range(halves)]
            center = [old[half, top, here, :] for half in range(halves)]
            gn = gs_ref[top - 1, here, :]
            for row in range(top, bottom):
                ge, gw, gs, di = (ge_ref[row, here, :], ge_ref[row, west, :], gs_ref[row, here, :], di_ref[row, here, :])
                for half in range(halves):
                    south = old[half, row + 1, here, :]
                    total = (ge * old[half, row, east, :] + gw * old[half, row, west, :]) + (
                        gs * south + gn * north[half]
                    )
                    new[half, row, here, :] = total * di
                    north[half], center[half] = center[half], south
                gn = gs
            return carry

        lax.fori_loop(1, cols // TILE + 3, apply, 0)
        for copy in copies(level + 1):
            copy.start()

    for half in range(halves):

        def gram(tile, sums, half=half):
            at = tile * TILE
            here = pl.ds(pl.multiple_of(at, TILE), TILE)
            east, west = pl.ds(at + 1, TILE), pl.ds(at - 1, TILE)
            sums = list(sums)
            for row in range(HALO, HALO + rows):
                ge, gw, gs, gn = (
                    ge_ref[row, here, :], ge_ref[row, west, :], gs_ref[row, here, :], gs_ref[row - 1, here, :],
                )
                last = (ge * v3[half, row, east, :] + gw * v3[half, row, west, :]) + (
                    gs * v3[half, row + 1, here, :] + gn * v3[half, row - 1, here, :]
                )
                dg = dg_ref[row, here, :]
                field = [ref[half, row, here, :] for ref in fields]
                image = [dg * value for value in field] + [last]
                number = 0
                for degree in range(2 * ITERS):
                    sums[number] += field[degree // 2] * image[degree - degree // 2]
                    number += 1
                for left in range(ITERS + 1):
                    for right in range(left, ITERS + 1):
                        sums[number] += image[left] * image[right]
                        number += 1
            return tuple(sums)

        count = 2 * ITERS + (ITERS + 1) * (ITERS + 2) // 2
        start = tuple(jnp.zeros((TILE, LANES), jnp.float32) for _ in range(count))
        sums = lax.fori_loop(first // TILE, (first + cols) // TILE, gram, start)
        lanes = slice(half * LANES, (half + 1) * LANES)
        for number in range(count):
            sums_ref[number : number + 1, lanes] = jnp.sum(sums[number], axis=0, keepdims=True)
        for number in range(count, SUMS):
            sums_ref[number : number + 1, lanes] = jnp.zeros((1, LANES), jnp.float32)
    for level in range(ITERS):
        for copy in copies(level):
            copy.wait()


def basis(pos, rhs, west, east, north, south, classes):
    rows, cols, scen = rhs.shape
    halves = scen // LANES
    tall, wide = rows + 2 * HALO, cols + 4 * TILE
    vmem = pl.BlockSpec(memory_space=pltpu.VMEM)
    field = jax.ShapeDtypeStruct((halves, rows, cols, LANES), jnp.float32)
    return pl.pallas_call(
        basis_kernel,
        in_specs=[pl.BlockSpec(memory_space=pltpu.SMEM)] + [vmem] * 6,
        out_specs=[pl.BlockSpec(memory_space=pl.ANY)] * ITERS + [vmem],
        out_shape=[field] * ITERS + [jax.ShapeDtypeStruct((SUMS, scen), jnp.float32)],
        scratch_shapes=[
            pltpu.VMEM((3, rows + 2 * TILE, 3 * LANES), jnp.float32),
            pltpu.VMEM((3 * LANES, LANES), jnp.float32),
        ]
        + [pltpu.VMEM((tall, wide, LANES), jnp.float32)] * 4
        + [pltpu.VMEM((halves, tall, wide, LANES), jnp.float32)] * ITERS
        + [pltpu.SemaphoreType.DMA((ITERS * halves,))],
        compiler_params=pltpu.CompilerParams(vmem_limit_bytes=56 * MIB),
    )(pos, rhs, west, east, north, south, classes)


def coefficients(moment, square):
    count = ITERS + 1

    def product(left, right):
        powers = {}
        for i, a in left.items():
            for j, b in right.items():
                powers[i + j] = powers[i + j] + a * b if i + j in powers else a * b
        total = None
        for power, value in powers.items():
            term = value * moment[power]
            total = term if total is None else total + term
        return total

    def norm(resid):
        total = None
        for i in range(count):
            for j in range(i, count):
                if i in resid and j in resid:
                    term = resid[i] * resid[j] * square[i, j]
                    term = term if i == j else 2.0 * term
                    total = term if total is None else total + term
        return jnp.sqrt(jnp.maximum(total, 0.0))

    def plus(left, factor, right):
        out = dict(left)
        for i, b in right.items():
            out[i] = out[i] + factor * b if i in out else factor * b
        return out

    one = jnp.ones_like(moment[0])
    resid, direction, solution = {0: one}, {0: one}, {}
    gamma = moment[0]
    norms = [jnp.sqrt(square[0, 0])]
    for iteration in range(ITERS):
        image = dict(direction)
        for i, value in direction.items():
            image[i + 1] = image[i + 1] - value if i + 1 in image else -value
        alpha = gamma / product(direction, image)
        solution = plus(solution, alpha, direction)
        resid = plus(resid, -alpha, image)
        norms.append(norm(resid))
        if iteration + 1 < ITERS:
            gamma_new = product(resid, resid)
            direction = plus(resid, gamma_new / gamma, direction)
            gamma = gamma_new
    return [solution[i] for i in range(ITERS)], norms


def combine_kernel(sums_ref, v0, v1, v2, v3, out_ref, norms_ref, factor_ref):
    halves, rows, cols, _ = v0.shape
    scen = halves * LANES

    @pl.when(pl.program_id(0) == 0)
    def _():
        line = lambda n: sums_ref[n : n + 1, :]
        moment = [line(n) for n in range(2 * ITERS)]
        square, number = {}, 2 * ITERS
        for i in range(ITERS + 1):
            for j in range(i, ITERS + 1):
                square[i, j] = line(number)
                number += 1
        factors, norms = coefficients(moment, square)
        for number, value in enumerate(factors):
            factor_ref[number : number + 1, :] = value
        stacked = jnp.concatenate(norms + [jnp.zeros((LANES - len(norms), scen), jnp.float32)], axis=0)
        norms_ref[...] = stacked.T[:, : len(norms)]

    flat = out_ref.reshape(scen * rows, cols)
    for row in range(rows):
        for half in range(halves):
            lanes = slice(half * LANES, (half + 1) * LANES)
            factor = [factor_ref[n : n + 1, lanes] for n in range(ITERS)]
            value = (factor[0] * v0[half, row] + factor[1] * v1[half, row]) + (
                factor[2] * v2[half, row] + factor[3] * v3[half, row]
            )
            flat[pl.ds(half * LANES * rows + row, LANES, stride=rows), :] = value.T


def combine(sums, fields):
    halves, rows, cols, _ = fields[0].shape
    scen = halves * LANES
    return pl.pallas_call(
        combine_kernel,
        grid=(rows // TILE,),
        in_specs=[pl.BlockSpec(sums.shape, lambda i: (0, 0))]
        + [pl.BlockSpec((halves, TILE, cols, LANES), lambda i: (0, i, 0, 0))] * ITERS,
        out_specs=[
            pl.BlockSpec((scen, TILE, cols), lambda i: (0, i, 0)),
            pl.BlockSpec((scen, ITERS + 1), lambda i: (0, 0)),
        ],
        out_shape=[
            jax.ShapeDtypeStruct((scen, rows, cols), jnp.float32),
            jax.ShapeDtypeStruct((scen, ITERS + 1), jnp.float32),
        ],
        scratch_shapes=[pltpu.VMEM((TILE, scen), jnp.float32)],
        compiler_params=pltpu.CompilerParams(vmem_limit_bytes=24 * MIB),
    )(sums, *fields)


def sum_everywhere(value):
    for axis in ("core", "z", "y", "x"):
        count = lax.axis_size(axis)
        for flip in (1,) if count == 2 else (1, 3):
            value = value + lax.ppermute(value, axis, [(i, i ^ flip) for i in range(count)])
    return value


def both_ways(to_low, to_high, axis):
    count = lax.axis_size(axis)
    up = [(i, i + 1) for i in range(count - 1)]
    return (
        lax.ppermute(to_high, axis, up),
        lax.ppermute(to_low, axis, [(b, a) for a, b in up]),
    )


def local(edge_h, edge_v, pads, loads, scales):
    rows, cols = pads.shape
    classes = jnp.concatenate([edge_h, edge_v, pads], axis=0).astype(jnp.float32)
    weights = -scales * jnp.asarray(load_table, jnp.float32)[None, :]
    table = jnp.pad(weights, ((0, 0), (0, LANES - weights.shape[1])))
    pos = jnp.stack(
        [
            lax.axis_index(ROW), lax.axis_index(COL),
            jnp.int32(rows * lax.axis_size(ROW)), jnp.int32(cols * lax.axis_size(COL)),
        ]
    ).astype(jnp.int32)
    rhs, to_west, to_east = prepare(loads, table, classes)
    west, east = both_ways(to_west, to_east, COL)
    to_north, to_south = messages(rhs, west, east, classes)
    north, south = both_ways(to_north, to_south, ROW)
    *fields, sums = basis(pos, rhs, west, east, north, south, classes)
    sums = sum_everywhere(sums)
    return tuple(combine(sums, fields))


def solution(mesh):
    finer = Mesh(mesh.devices.reshape(4, 2, 4, 4), ("x", "core", "y", "z"))
    in_specs = (P(ROW, COL), P(ROW, COL), P(ROW, COL), P(None, ROW, COL), P())
    out_specs = (P(None, ROW, COL), P())
    return jax.shard_map(local, mesh=finer, in_specs=in_specs, out_specs=out_specs, check_vma=False)
```

```python
import jax
import jax.numpy as jnp
from jax import lax
from jax.experimental import pallas as pl
from jax.experimental.pallas import tpu as pltpu
from jax.sharding import Mesh
from jax.sharding import PartitionSpec as P

ITERS = 4
ROW = ("x", "core")
COL = ("y", "z")

edge_table = (0.5, 0.8, 1.2, 1.7, 2.3, 3.0, 3.8, 4.7)
load_table = (0.25, 0.5, 1.0, 1.5, 2.0, 3.0, 4.0, 6.0)
pad_conductance = 20.0
leakage = 0.05

LANES = 128
TILE = 8
HALO = ITERS
FIRST = 2 * TILE
LEFT = TILE
COUNT = 2 * ITERS + (ITERS + 1) * (ITERS + 2) // 2
SUMS = 24
MIB = 1024 * 1024
ON_CHIP = pl.BlockSpec(memory_space=pltpu.VMEM)
IN_HBM = pl.BlockSpec(memory_space=pltpu.HBM)


def resident(*shape):
    return pltpu.VMEM(shape, jnp.float32)


def lookup(classes, table):
    total = jnp.zeros(classes.shape, jnp.float32)
    for number, amount in enumerate(table):
        total = total + jnp.where(classes == number, jnp.float32(amount), jnp.float32(0.0))
    return total


def is_even(axes):
    return lax.axis_index(axes[-1]) % 2 == 0


def half_lanes(half):
    return slice(half * LANES, (half + 1) * LANES)


def put(first, second, even, index, low, high):
    first[index] = jnp.where(even, high, low)
    second[index] = jnp.where(even, low, high)


def get(first, second, even, index):
    a, b = first[index], second[index]
    return jnp.where(even, b, a), jnp.where(even, a, b)


def swaps(first, second, axes):
    count = 1
    for axis in axes:
        count *= lax.axis_size(axis)
    later = [(i, i + 1) for i in range(1, count - 1, 2)]
    return (
        lax.ppermute(first, axes, [(i, i ^ 1) for i in range(count)]),
        lax.ppermute(second, axes, later + [(b, a) for a, b in later]),
    )


def prepare_kernel(loads_hbm, scales_ref, eh_ref, ev_ref, pads_ref, rhs_ref, turned_ref, first_ref, second_ref, buf, table_ref, sem):
    scen, rows, cols = loads_hbm.shape
    chunks = rows // TILE

    def copy(chunk):
        source = loads_hbm.at[:, chunk * TILE : (chunk + 1) * TILE, :]
        return pltpu.make_async_copy(source, buf.at[chunk], sem.at[chunk])

    for chunk in range(chunks):
        copy(chunk).start()
    even = is_even(COL)
    classes = jnp.concatenate([eh_ref[...], ev_ref[...], pads_ref[...]], axis=0).astype(jnp.float32)
    classes = jnp.concatenate([classes, jnp.zeros((LANES - 3 * rows, cols), jnp.float32)], axis=0)
    turned_ref[...] = classes.T
    low, high = turned_ref[:TILE, :], turned_ref[cols - TILE :, :]
    put(first_ref, second_ref, even, (rows // 2, slice(None), half_lanes(0)), low, high)
    put(first_ref, second_ref, even, (rows // 2, slice(None), half_lanes(1)), low, high)
    weights = jnp.concatenate(
        [-scales_ref[n : n + 1, :] * jnp.float32(load_table[n]) for n in range(len(load_table))], axis=0
    )
    weights = jnp.concatenate([weights, jnp.zeros((LANES - len(load_table), scen), jnp.float32)], axis=0)
    for half in range(scen // LANES):
        table_ref[half_lanes(half), :] = weights[:, half_lanes(half)].T
    for chunk in range(chunks):
        copy(chunk).wait()
        flat = buf.at[chunk].reshape(scen * TILE, cols)
        for inner in range(TILE):
            row = chunk * TILE + inner
            for half in range(scen // LANES):
                index = flat[pl.ds(half * LANES * TILE + inner, LANES, stride=TILE), :]
                value = jnp.take_along_axis(table_ref[half_lanes(half), :], index, axis=1).T
                rhs_ref[row, :, half_lanes(half)] = value
                at = (row // 2, slice(row % 2 * HALO, (row % 2 + 1) * HALO), half_lanes(half))
                put(first_ref, second_ref, even, at, value[:HALO], value[cols - HALO :])


def prepare(loads, scales, edge_h, edge_v, pads):
    scen, rows, cols = loads.shape
    side = resident(rows // 2 + 1, TILE, scen)
    return pl.pallas_call(
        prepare_kernel,
        in_specs=[IN_HBM] + [ON_CHIP] * 4,
        out_specs=[ON_CHIP] * 4,
        out_shape=[resident(rows, cols, scen), resident(cols, LANES), side, side],
        scratch_shapes=[
            pltpu.VMEM((rows // TILE, scen, TILE, cols), jnp.int32),
            pltpu.VMEM((scen, LANES), jnp.float32),
            pltpu.SemaphoreType.DMA((rows // TILE,)),
        ],
        compiler_params=pltpu.CompilerParams(vmem_limit_bytes=12 * MIB),
        cost_estimate=pl.CostEstimate(flops=20_000_000, bytes_accessed=12 * MIB, transcendentals=0),
    )(loads, scales, edge_h, edge_v, pads)


def message_kernel(rhs_ref, turned_ref, side_a, side_b, first_ref, second_ref):
    rows, cols, scen = rhs_ref.shape
    across = cols // TILE + 1
    even_row, even_col = is_even(ROW), is_even(COL)

    def corner(row, lanes):
        west, east = get(side_a, side_b, even_col, (row // 2, slice(row % 2 * HALO, (row % 2 + 1) * HALO), lanes))
        return jnp.concatenate([east, west], axis=0)

    for row in range(HALO):
        blocks = slice(row * across, row * across + across - 1)
        for half in range(scen // LANES):
            lanes = half_lanes(half)
            low = rhs_ref[row, :, lanes].reshape(across - 1, TILE, LANES)
            high = rhs_ref[rows - HALO + row, :, lanes].reshape(across - 1, TILE, LANES)
            put(first_ref, second_ref, even_row, (blocks, slice(None), lanes), low, high)
            at = (row * across + across - 1, slice(None), lanes)
            put(first_ref, second_ref, even_row, at, corner(row, lanes), corner(rows - HALO + row, lanes))
    west, east = get(side_a, side_b, even_col, (rows // 2, slice(None), half_lanes(0)))
    tiles = [west] + [turned_ref[n * TILE : (n + 1) * TILE, :] for n in range(cols // TILE)] + [east]
    for number, tile in enumerate(tiles):
        at = (HALO * across + number // 2, slice(None), half_lanes(number % 2))
        first_ref[at] = tile
        second_ref[at] = tile


def messages(rhs, turned, side_a, side_b):
    rows, cols, scen = rhs.shape
    tiles = cols // TILE
    out = resident(HALO * (tiles + 1) + (tiles + 2) // 2, TILE, scen)
    return pl.pallas_call(
        message_kernel,
        in_specs=[ON_CHIP] * 4,
        out_specs=[ON_CHIP] * 2,
        out_shape=[out, out],
        compiler_params=pltpu.CompilerParams(vmem_limit_bytes=4 * MIB),
    )(rhs, turned, side_a, side_b)


def conductances(grid, rows, turned_ref, west=None, east=None, north=None, south=None):
    cols = turned_ref.shape[0]
    blank = jnp.zeros((TILE, LANES), jnp.float32)
    side = [blank if piece is None else piece for piece in (west, east)]
    own = jnp.concatenate([blank, side[0], turned_ref[...], side[1], blank], axis=0)
    shape = own.shape
    lane = lax.broadcasted_iota(jnp.int32, shape, 1)

    def classes(array):
        out = pltpu.roll(own, (LEFT - array * rows) % LANES, 1)
        if north is not None:
            above = pltpu.roll(north, (LEFT - (array + 1) * rows) % LANES, 1)
            below = pltpu.roll(south, (LEFT + rows - array * rows) % LANES, 1)
            out = jnp.where(lane < LEFT, above, jnp.where(lane < LEFT + rows, out, below))
        return out

    row_ids = lax.axis_index(ROW) * rows - LEFT + lane
    col_ids = lax.axis_index(COL) * cols - FIRST + lax.broadcasted_iota(jnp.int32, shape, 0)
    all_rows, all_cols = grid
    inside = (row_ids >= 0) & (row_ids < all_rows) & (col_ids >= 0) & (col_ids < all_cols)
    zero = jnp.zeros(shape, jnp.float32)
    g_east = jnp.where(inside & (col_ids < all_cols - 1), lookup(classes(0), edge_table), zero)
    g_south = jnp.where(inside & (row_ids < all_rows - 1), lookup(classes(1), edge_table), zero)
    g_west = pltpu.roll(g_east, 1, 0)
    g_north = pltpu.roll(g_south, 1, 1)
    diagonal = g_east + g_west + g_south + g_north + classes(2) * pad_conductance + leakage
    return g_east, g_south, 1.0 / diagonal, diagonal


def tile_at(tile):
    return pl.ds(pl.multiple_of(tile * TILE, TILE), TILE)


def over(tiles, body):
    if isinstance(tiles, range):
        lax.fori_loop(tiles.start, tiles.stop, lambda tile, carry: (body(tile), carry)[1], 0)
    else:
        for tile in tiles:
            body(tile)


def spread(value, scratch, out, rows, tiles):
    scratch[...] = value

    def body(tile):
        piece = scratch[tile_at(tile), :]
        for row in rows:
            lane = LEFT + row
            out[HALO + row, tile_at(tile), :] = jnp.broadcast_to(piece[:, lane : lane + 1], (TILE, LANES))

    over(tiles, body)


def step(old, new, coef, runs, tiles):
    ge_ref, gs_ref, di_ref, _ = coef
    halves = old.shape[0]

    def body(tile):
        at = tile * TILE
        here, east, west = tile_at(tile), pl.ds(at + 1, TILE), pl.ds(at - 1, TILE)
        for run in runs:
            top = HALO + run[0]
            north = [old[half, top - 1, here, :] for half in range(halves)]
            center = [old[half, top, here, :] for half in range(halves)]
            gn = gs_ref[top - 1, here, :]
            for row in range(top, top + len(run)):
                ge, gw = ge_ref[row, here, :], ge_ref[row, west, :]
                gs, di = gs_ref[row, here, :], di_ref[row, here, :]
                for half in range(halves):
                    south = old[half, row + 1, here, :]
                    total = (ge * old[half, row, east, :] + gw * old[half, row, west, :]) + (
                        gs * south + gn * north[half]
                    )
                    new[half, row, here, :] = total * di
                    north[half], center[half] = center[half], south
                gn = gs

    over(tiles, body)


def gram(fields, coef, half, rows, tiles, sums):
    ge_ref, gs_ref, _, dg_ref = coef
    v = fields[-1]

    def body(tile, sums):
        at = tile * TILE
        here, east, west = tile_at(tile), pl.ds(at + 1, TILE), pl.ds(at - 1, TILE)
        sums = list(sums)
        for own in rows:
            row = HALO + own
            last = (
                ge_ref[row, here, :] * v[half, row, east, :] + ge_ref[row, west, :] * v[half, row, west, :]
            ) + (gs_ref[row, here, :] * v[half, row + 1, here, :] + gs_ref[row - 1, here, :] * v[half, row - 1, here, :])
            dg = dg_ref[row, here, :]
            field = [ref[half, row, here, :] for ref in fields]
            image = [dg * value for value in field] + [last]
            number = 0
            for degree in range(2 * ITERS):
                sums[number] += field[degree // 2] * image[degree - degree // 2]
                number += 1
            for i in range(ITERS + 1):
                for j in range(i, ITERS + 1):
                    sums[number] += image[i] * image[j]
                    number += 1
        return tuple(sums)

    return lax.fori_loop(tiles.start, tiles.stop, body, tuple(sums))


def own_kernel(grid, rhs_ref, turned_ref, ge_ref, gs_ref, di_ref, dg_ref, v0, scratch):
    rows, cols, scen = rhs_ref.shape
    tiles = range(FIRST // TILE, FIRST // TILE + cols // TILE)
    later, below = range(tiles.start + 1, tiles.stop), range(1, rows)
    ge, gs, di, dg = conductances(grid, rows, turned_ref)
    spread(ge, scratch, ge_ref, range(rows), tiles)
    spread(gs, scratch, gs_ref, range(rows), tiles)
    spread(di, scratch, di_ref, below, later)
    spread(dg, scratch, dg_ref, below, later)
    start_own(rhs_ref, di_ref, v0, below, later)


def start_own(rhs_ref, di_ref, v0, rows, tiles):
    def body(tile):
        for row in rows:
            di = di_ref[HALO + row, tile_at(tile), :]
            for half in range(v0.shape[0]):
                value = rhs_ref[row, tile_at(tile - FIRST // TILE), half_lanes(half)]
                v0[half, HALO + row, tile_at(tile), :] = value * di

    over(tiles, body)


def start_side(side_a, side_b, di_ref, v0, rows, cols):
    even = is_even(COL)
    for row in rows:
        for half in range(v0.shape[0]):
            at = (row // 2, slice(row % 2 * HALO, (row % 2 + 1) * HALO), half_lanes(half))
            west, east = get(side_a, side_b, even, at)
            for piece, start in ((west, FIRST - HALO), (east, FIRST + cols)):
                where = slice(start, start + HALO)
                v0[half, HALO + row, where, :] = piece * di_ref[HALO + row, where, :]


def inner_kernel(
    grid, rhs_ref, turned_ref, side_a, side_b, *refs
):
    (ge_ref, gs_ref, di_ref, dg_ref, v0, v1, v2, v3, sums_ref, scratch) = refs[5:]
    coef, fields = (ge_ref, gs_ref, di_ref, dg_ref), (v0, v1, v2, v3)
    rows, cols, scen = rhs_ref.shape
    own = range(FIRST // TILE, FIRST // TILE + cols // TILE)
    low, high = own.start - 1, own.stop
    below = range(1, rows)
    west, east = get(side_a, side_b, is_even(COL), (rows // 2, slice(None), half_lanes(0)))
    ge, gs, di, dg = conductances(grid, rows, turned_ref, west, east)
    spread(ge, scratch, ge_ref, range(rows), (low, high))
    spread(gs, scratch, gs_ref, range(rows), (low, high))
    spread(di, scratch, di_ref, below, (low, own.start, high))
    spread(dg, scratch, dg_ref, below, (own.start,))
    start_own(rhs_ref, di_ref, v0, below, (own.start,))
    start_side(side_a, side_b, di_ref, v0, below, cols)
    for level in range(1, ITERS):
        run = range(1 + level, rows - level)
        step(fields[level - 1], fields[level], coef, (run,), range(low, high + 1))
    for half in range(scen // LANES):
        sums = [jnp.zeros((TILE, LANES), jnp.float32)] * COUNT
        sums = gram(fields, coef, half, range(1 + ITERS, rows - ITERS), own, sums)
        for number, value in enumerate(sums):
            sums_ref[half, number] = value


def outer_kernel(
    grid, rhs_ref, turned_ref, side_a, side_b, end_a, end_b, inner_ref, *refs
):
    (ge_ref, gs_ref, di_ref, dg_ref, v0, v1, v2, v3, sums_ref, scratch) = refs[8:]
    coef, fields = (ge_ref, gs_ref, di_ref, dg_ref), (v0, v1, v2, v3)
    rows, cols, scen = rhs_ref.shape
    own = range(FIRST // TILE, FIRST // TILE + cols // TILE)
    reach = range(own.start - 1, own.stop + 1)
    across = cols // TILE + 1
    even_row = is_even(ROW)
    west, east = get(side_a, side_b, is_even(COL), (rows // 2, slice(None), half_lanes(0)))
    blank = jnp.zeros((TILE, LANES), jnp.float32)
    ends = [[blank], [blank]]
    for number in range(cols // TILE + 2):
        at = (HALO * across + number // 2, slice(None), half_lanes(number % 2))
        for pieces, value in zip(ends, get(end_a, end_b, even_row, at), strict=True):
            pieces.append(value)
    north, south = (jnp.concatenate(pieces + [blank], axis=0) for pieces in ends)
    above, under = range(-HALO, 0), range(rows, rows + HALO)
    ge, gs, di, dg = conductances(grid, rows, turned_ref, west, east, north, south)
    outside = (*above, *under)
    spread(ge, scratch, ge_ref, outside, reach)
    spread(gs, scratch, gs_ref, outside, reach)
    spread(di, scratch, di_ref, (*above, 0, *under), reach)
    spread(dg, scratch, dg_ref, (0,), own)
    start_own(rhs_ref, di_ref, v0, (0,), own)
    start_side(side_a, side_b, di_ref, v0, (0,), cols)
    for number in range(HALO):
        for half in range(scen // LANES):

            def fill(tile, carry, number=number, half=half):
                block = number * across + jnp.where(tile == reach.start, across - 1, tile - own.start)
                pair = get(end_a, end_b, even_row, (block, slice(None), half_lanes(half)))
                for value, row in zip(pair, (HALO + above[number], HALO + under[number]), strict=True):
                    v0[half, row, tile_at(tile), :] = value * di_ref[row, tile_at(tile), :]
                return carry

            lax.fori_loop(reach.start, reach.stop, fill, 0)
    for level in range(1, ITERS):
        runs = (range(level - HALO, level + 1), range(rows - level, rows + HALO - level))
        step(fields[level - 1], fields[level], coef, runs, reach)
    for half in range(scen // LANES):
        sums = [inner_ref[half, number] for number in range(COUNT)]
        sums = gram(fields, coef, half, (*range(ITERS + 1), *range(rows - ITERS, rows)), own, sums)
        for number in range(SUMS):
            value = jnp.sum(sums[number], axis=0, keepdims=True) if number < COUNT else jnp.zeros((1, LANES))
            sums_ref[number : number + 1, half_lanes(half)] = value


def basis(grid, rhs, turned, side):
    rows, cols, scen = rhs.shape
    halves = scen // LANES
    tall, wide = rows + 2 * HALO, cols + 4 * TILE
    coef = [resident(tall, wide, LANES)] * 4
    field = resident(halves, tall, wide, LANES)
    scratch = [pltpu.VMEM((wide, LANES), jnp.float32)]
    params = pltpu.CompilerParams(vmem_limit_bytes=4 * MIB)

    def cost(microseconds):
        return pl.CostEstimate(flops=0, bytes_accessed=int(microseconds * 3.0e6), transcendentals=0)

    *coefs, v0 = pl.pallas_call(
        lambda *refs: own_kernel(grid, *refs),
        in_specs=[ON_CHIP] * 2,
        out_specs=[ON_CHIP] * 5,
        out_shape=coef + [field],
        scratch_shapes=scratch,
        compiler_params=params,
        cost_estimate=cost(8),
    )(rhs, turned)
    partial = resident(halves, SUMS, TILE, LANES)
    *coefs, v0, v1, v2, v3, sums = pl.pallas_call(
        lambda *refs: inner_kernel(grid, *refs),
        in_specs=[ON_CHIP] * 9,
        out_specs=[ON_CHIP] * 9,
        out_shape=coef + [field] * ITERS + [partial],
        scratch_shapes=scratch,
        input_output_aliases={4 + n: n for n in range(5)},
        compiler_params=params,
        cost_estimate=cost(14),
    )(rhs, turned, *side, *coefs, v0)

    def finish(end):
        state = [*coefs, v0, v1, v2, v3]
        *out, total = pl.pallas_call(
            lambda *refs: outer_kernel(grid, *refs),
            in_specs=[ON_CHIP] * 15,
            out_specs=[ON_CHIP] * 9,
            out_shape=coef + [field] * ITERS + [resident(SUMS, scen)],
            scratch_shapes=scratch,
            input_output_aliases={7 + n: n for n in range(8)},
            compiler_params=params,
            cost_estimate=cost(7),
        )(rhs, turned, *side, *end, sums, *state)
        return out[4:], total

    return finish


def coefficients(moment, square):
    count = ITERS + 1

    def product(left, right):
        powers = {}
        for i, a in left.items():
            for j, b in right.items():
                powers[i + j] = powers[i + j] + a * b if i + j in powers else a * b
        total = None
        for power, value in powers.items():
            term = value * moment[power]
            total = term if total is None else total + term
        return total

    def norm(resid):
        total = None
        for i in range(count):
            for j in range(i, count):
                if i in resid and j in resid:
                    term = resid[i] * resid[j] * square[i, j]
                    term = term if i == j else 2.0 * term
                    total = term if total is None else total + term
        return jnp.sqrt(jnp.maximum(total, 0.0))

    def plus(left, factor, right):
        out = dict(left)
        for i, b in right.items():
            out[i] = out[i] + factor * b if i in out else factor * b
        return out

    one = jnp.ones_like(moment[0])
    resid, direction, solution = {0: one}, {0: one}, {}
    gamma = moment[0]
    norms = [jnp.sqrt(square[0, 0])]
    for iteration in range(ITERS):
        image = dict(direction)
        for i, value in direction.items():
            image[i + 1] = image[i + 1] - value if i + 1 in image else -value
        alpha = gamma / product(direction, image)
        solution = plus(solution, alpha, direction)
        resid = plus(resid, -alpha, image)
        norms.append(norm(resid))
        if iteration + 1 < ITERS:
            gamma_new = product(resid, resid)
            direction = plus(resid, gamma_new / gamma, direction)
            gamma = gamma_new
    return [solution[i] for i in range(ITERS)], norms


def combine_kernel(sums_ref, v0, v1, v2, v3, out_hbm, norms_ref, factor_ref, buf, sem):
    scen, rows, cols = out_hbm.shape
    line = lambda n: sums_ref[n : n + 1, :]
    moment = [line(n) for n in range(2 * ITERS)]
    square, number = {}, 2 * ITERS
    for i in range(ITERS + 1):
        for j in range(i, ITERS + 1):
            square[i, j] = line(number)
            number += 1
    factors, norms = coefficients(moment, square)
    for number, value in enumerate(factors):
        factor_ref[number : number + 1, :] = value
    for number, value in enumerate(norms):
        norms_ref[number : number + 1, :] = value

    def copy(chunk):
        target = out_hbm.at[:, chunk * TILE : (chunk + 1) * TILE, :]
        return pltpu.make_async_copy(buf.at[chunk], target, sem.at[chunk])

    for chunk in range(rows // TILE):
        flat = buf.at[chunk].reshape(scen * TILE, cols)
        for inner in range(TILE):
            row = HALO + chunk * TILE + inner
            for half in range(scen // LANES):
                factor = [factor_ref[n : n + 1, half_lanes(half)] for n in range(ITERS)]
                part = [f * v[half, row, FIRST : FIRST + cols, :] for f, v in zip(factor, (v0, v1, v2, v3), strict=True)]
                value = (part[0] + part[1]) + (part[2] + part[3])
                flat[pl.ds(half * LANES * TILE + inner, LANES, stride=TILE), :] = value.T
        copy(chunk).start()
    for chunk in range(rows // TILE):
        copy(chunk).wait()


def combine(sums, fields, scen, rows, cols):
    drop, norms = pl.pallas_call(
        combine_kernel,
        in_specs=[ON_CHIP] * 5,
        out_specs=[IN_HBM, ON_CHIP],
        out_shape=[
            jax.ShapeDtypeStruct((scen, rows, cols), jnp.float32),
            jax.ShapeDtypeStruct((ITERS + 1, scen), jnp.float32),
        ],
        scratch_shapes=[
            pltpu.VMEM((TILE, scen), jnp.float32),
            pltpu.VMEM((rows // TILE, scen, TILE, cols), jnp.float32),
            pltpu.SemaphoreType.DMA((rows // TILE,)),
        ],
        compiler_params=pltpu.CompilerParams(vmem_limit_bytes=8 * MIB),
    )(sums, *fields)
    return drop, norms.T


def sum_everywhere(value):
    for axis in ("core", "z", "y", "x"):
        count = lax.axis_size(axis)
        for flip in (1,) if count == 2 else (1, 3):
            value = value + lax.ppermute(value, axis, [(i, i ^ flip) for i in range(count)])
    return value


def local(edge_h, edge_v, pads, loads, scales):
    scen, rows, cols = loads.shape
    grid = (rows * lax.axis_size(ROW), cols * lax.axis_size(COL))
    rhs, turned, *side = prepare(loads, scales.T, edge_h, edge_v, pads)
    side = swaps(*side, COL)
    finish = basis(grid, rhs, turned, side)
    end = swaps(*messages(rhs, turned, *side), ROW)
    fields, sums = finish(end)
    return combine(sum_everywhere(sums), fields, scen, rows, cols)


def solution(mesh):
    finer = Mesh(mesh.devices.reshape(4, 2, 4, 4), ("x", "core", "y", "z"))
    in_specs = (P(ROW, COL), P(ROW, COL), P(ROW, COL), P(None, ROW, COL), P())
    out_specs = (P(None, ROW, COL), P())
    return jax.shard_map(local, mesh=finer, in_specs=in_specs, out_specs=out_specs, check_vma=False)
```

```python
import jax
import jax.numpy as jnp
from jax import lax
from jax.experimental import pallas as pl
from jax.experimental.pallas import tpu as pltpu
from jax.sharding import Mesh
from jax.sharding import PartitionSpec as P

ITERS = 4
ROW = ("x", "core")
COL = ("y", "z")

edge_table = (0.5, 0.8, 1.2, 1.7, 2.3, 3.0, 3.8, 4.7)
load_table = (0.25, 0.5, 1.0, 1.5, 2.0, 3.0, 4.0, 6.0)
pad_conductance = 20.0
leakage = 0.05

LANES = 128
TILE = 8
HALO = ITERS
FIRST = 2 * TILE
LEFT = TILE
COUNT = 2 * ITERS + (ITERS + 1) * (ITERS + 2) // 2
SUMS = 24
MIB = 1024 * 1024
ON_CHIP = pl.BlockSpec(memory_space=pltpu.VMEM)
IN_HBM = pl.BlockSpec(memory_space=pltpu.HBM)


def resident(*shape):
    return pltpu.VMEM(shape, jnp.float32)


def lookup(classes, table):
    total = jnp.zeros(classes.shape, jnp.float32)
    for number, amount in enumerate(table):
        total = total + jnp.where(classes == number, jnp.float32(amount), jnp.float32(0.0))
    return total


def is_even(axes):
    return lax.axis_index(axes[-1]) % 2 == 0


def half_lanes(half):
    return slice(half * LANES, (half + 1) * LANES)


def put(first, second, even, index, low, high):
    first[index] = jnp.where(even, high, low)
    second[index] = jnp.where(even, low, high)


def get(first, second, even, index):
    a, b = first[index], second[index]
    return jnp.where(even, b, a), jnp.where(even, a, b)


def swaps(first, second, axes):
    count = 1
    for axis in axes:
        count *= lax.axis_size(axis)
    later = [(i, i + 1) for i in range(1, count - 1, 2)]
    return (
        lax.ppermute(first, axes, [(i, i ^ 1) for i in range(count)]),
        lax.ppermute(second, axes, later + [(b, a) for a, b in later]),
    )


def pick(table, classes):
    bit = 1
    while len(table) > 1:
        odd = (classes & bit) != 0
        table = [jnp.where(odd, table[n + 1], table[n]) for n in range(0, len(table), 2)]
        bit *= 2
    return table[0]


def prepare_kernel(
    loads_hbm, scales_hbm, eh_hbm, ev_hbm, pads_hbm, rhs_ref, turned_ref, first_ref, second_ref,
    buf, scales_ref, classes_ref, sem, small_sem,
):
    scen, rows, cols = loads_hbm.shape
    chunks = rows // TILE
    small = [pltpu.make_async_copy(scales_hbm, scales_ref, small_sem.at[3])]
    for array, source in enumerate((eh_hbm, ev_hbm, pads_hbm)):
        target = classes_ref.at[array * rows : (array + 1) * rows, :]
        small.append(pltpu.make_async_copy(source, target, small_sem.at[array]))
    for one in small:
        one.start()

    def copy(chunk):
        source = loads_hbm.at[:, chunk * TILE : (chunk + 1) * TILE, :]
        return pltpu.make_async_copy(source, buf.at[chunk], sem.at[chunk])

    for chunk in range(chunks):
        copy(chunk).start()
    even = is_even(COL)
    for one in small:
        one.wait()
    classes = classes_ref[...].astype(jnp.float32)
    classes = jnp.concatenate([classes, jnp.zeros((LANES - 3 * rows, cols), jnp.float32)], axis=0)
    turned_ref[...] = classes.T
    low, high = turned_ref[:TILE, :], turned_ref[cols - TILE :, :]
    put(first_ref, second_ref, even, (rows // 2, slice(None), half_lanes(0)), low, high)
    put(first_ref, second_ref, even, (rows // 2, slice(None), half_lanes(1)), low, high)
    weights = jnp.concatenate(
        [-scales_ref[n : n + 1, :] * jnp.float32(load_table[n]) for n in range(len(load_table))], axis=0
    )
    for chunk in range(chunks):
        copy(chunk).wait()
        flat = buf.at[chunk].reshape(scen * TILE, cols)
        for inner in range(TILE):
            row = chunk * TILE + inner
            for half in range(scen // LANES):
                index = flat[pl.ds(half * LANES * TILE + inner, LANES, stride=TILE), :]
                value = pick([weights[n : n + 1, half_lanes(half)] for n in range(8)], index.T)
                rhs_ref[row, :, half_lanes(half)] = value
                at = (row // 2, slice(row % 2 * HALO, (row % 2 + 1) * HALO), half_lanes(half))
                put(first_ref, second_ref, even, at, value[:HALO], value[cols - HALO :])


def prepare(loads, scales, edge_h, edge_v, pads):
    scen, rows, cols = loads.shape
    side = resident(rows // 2 + 1, TILE, scen)
    return pl.pallas_call(
        prepare_kernel,
        in_specs=[IN_HBM] * 5,
        out_specs=[ON_CHIP] * 4,
        out_shape=[resident(rows, cols, scen), resident(cols, LANES), side, side],
        scratch_shapes=[
            pltpu.VMEM((rows // TILE, scen, TILE, cols), jnp.int32),
            pltpu.VMEM(scales.shape, jnp.float32),
            pltpu.VMEM((3 * rows, cols), jnp.int32),
            pltpu.SemaphoreType.DMA((rows // TILE,)),
            pltpu.SemaphoreType.DMA((4,)),
        ],
        compiler_params=pltpu.CompilerParams(vmem_limit_bytes=12 * MIB),
        cost_estimate=pl.CostEstimate(flops=20_000_000, bytes_accessed=12 * MIB, transcendentals=0),
    )(*(pltpu.with_memory_space_constraint(a, pltpu.HBM) for a in (loads, scales, edge_h, edge_v, pads)))


def message_kernel(rhs_ref, turned_ref, side_a, side_b, _, first_ref, second_ref):
    rows, cols, scen = rhs_ref.shape
    across = cols // TILE + 1
    even_row, even_col = is_even(ROW), is_even(COL)

    def corner(row, lanes):
        west, east = get(side_a, side_b, even_col, (row // 2, slice(row % 2 * HALO, (row % 2 + 1) * HALO), lanes))
        return jnp.concatenate([east, west], axis=0)

    for row in range(HALO):
        blocks = slice(row * across, row * across + across - 1)
        for half in range(scen // LANES):
            lanes = half_lanes(half)
            low = rhs_ref[row, :, lanes].reshape(across - 1, TILE, LANES)
            high = rhs_ref[rows - HALO + row, :, lanes].reshape(across - 1, TILE, LANES)
            put(first_ref, second_ref, even_row, (blocks, slice(None), lanes), low, high)
            at = (row * across + across - 1, slice(None), lanes)
            put(first_ref, second_ref, even_row, at, corner(row, lanes), corner(rows - HALO + row, lanes))
    west, east = get(side_a, side_b, even_col, (rows // 2, slice(None), half_lanes(0)))
    tiles = [west] + [turned_ref[n * TILE : (n + 1) * TILE, :] for n in range(cols // TILE)] + [east]
    for number, tile in enumerate(tiles):
        at = (HALO * across + number // 2, slice(None), half_lanes(number % 2))
        first_ref[at] = tile
        second_ref[at] = tile


def messages(rhs, turned, side_a, side_b, after):
    rows, cols, scen = rhs.shape
    tiles = cols // TILE
    out = resident(HALO * (tiles + 1) + (tiles + 2) // 2, TILE, scen)
    return pl.pallas_call(
        message_kernel,
        in_specs=[ON_CHIP] * 5,
        out_specs=[ON_CHIP] * 2,
        out_shape=[out, out],
        compiler_params=pltpu.CompilerParams(vmem_limit_bytes=4 * MIB),
    )(rhs, turned, side_a, side_b, after)


def conductances(grid, rows, turned_ref, west=None, east=None, north=None, south=None):
    cols = turned_ref.shape[0]
    blank = jnp.zeros((TILE, LANES), jnp.float32)
    side = [blank if piece is None else piece for piece in (west, east)]
    own = jnp.concatenate([blank, side[0], turned_ref[...], side[1], blank], axis=0)
    shape = own.shape
    lane = lax.broadcasted_iota(jnp.int32, shape, 1)

    def classes(array):
        out = pltpu.roll(own, (LEFT - array * rows) % LANES, 1)
        if north is not None:
            above = pltpu.roll(north, (LEFT - (array + 1) * rows) % LANES, 1)
            below = pltpu.roll(south, (LEFT + rows - array * rows) % LANES, 1)
            out = jnp.where(lane < LEFT, above, jnp.where(lane < LEFT + rows, out, below))
        return out

    row_ids = lax.axis_index(ROW) * rows - LEFT + lane
    col_ids = lax.axis_index(COL) * cols - FIRST + lax.broadcasted_iota(jnp.int32, shape, 0)
    all_rows, all_cols = grid
    inside = (row_ids >= 0) & (row_ids < all_rows) & (col_ids >= 0) & (col_ids < all_cols)
    zero = jnp.zeros(shape, jnp.float32)
    g_east = jnp.where(inside & (col_ids < all_cols - 1), lookup(classes(0), edge_table), zero)
    g_south = jnp.where(inside & (row_ids < all_rows - 1), lookup(classes(1), edge_table), zero)
    g_west = pltpu.roll(g_east, 1, 0)
    g_north = pltpu.roll(g_south, 1, 1)
    diagonal = g_east + g_west + g_south + g_north + classes(2) * pad_conductance + leakage
    return g_east, g_south, 1.0 / diagonal, diagonal


def tile_at(tile):
    if isinstance(tile, int):
        return slice(tile * TILE, (tile + 1) * TILE)
    return pl.ds(pl.multiple_of(tile * TILE, TILE), TILE)


def over(tiles, body, together=1):
    if len(tiles) <= together:
        for tile in tiles:
            body(tile)
        return

    def turn(number, carry):
        for extra in range(together):
            body(tiles.start + number * together + extra)
        return carry

    lax.fori_loop(0, len(tiles) // together, turn, 0)


def spread(value, out, rows, tiles):
    for tile in tiles:
        piece = value[tile * TILE : (tile + 1) * TILE, :]
        for row in rows:
            lane = LEFT + row
            out[HALO + row, tile_at(tile), :] = jnp.broadcast_to(piece[:, lane : lane + 1], (TILE, LANES))


def step(old, new, coef, runs, tiles, together=1):
    ge_ref, gs_ref, di_ref, _ = coef
    halves = old.shape[0]

    def body(tile):
        at = tile * TILE
        here, east, west = tile_at(tile), pl.ds(at + 1, TILE), pl.ds(at - 1, TILE)
        for run in runs:
            top = HALO + run[0]
            north = [old[half, top - 1, here, :] for half in range(halves)]
            center = [old[half, top, here, :] for half in range(halves)]
            gn = gs_ref[top - 1, here, :]
            for row in range(top, top + len(run)):
                ge, gw = ge_ref[row, here, :], ge_ref[row, west, :]
                gs, di = gs_ref[row, here, :], di_ref[row, here, :]
                for half in range(halves):
                    south = old[half, row + 1, here, :]
                    total = (ge * old[half, row, east, :] + gw * old[half, row, west, :]) + (
                        gs * south + gn * north[half]
                    )
                    new[half, row, here, :] = total * di
                    north[half], center[half] = center[half], south
                gn = gs

    over(tiles, body, together)


def gram(fields, coef, half, rows, tiles, sums):
    ge_ref, gs_ref, _, dg_ref = coef
    v = fields[-1]

    def body(tile, sums):
        at = tile * TILE
        here, east, west = tile_at(tile), pl.ds(at + 1, TILE), pl.ds(at - 1, TILE)
        sums = list(sums)
        for own in rows:
            row = HALO + own
            last = (
                ge_ref[row, here, :] * v[half, row, east, :] + ge_ref[row, west, :] * v[half, row, west, :]
            ) + (gs_ref[row, here, :] * v[half, row + 1, here, :] + gs_ref[row - 1, here, :] * v[half, row - 1, here, :])
            dg = dg_ref[row, here, :]
            field = [ref[half, row, here, :] for ref in fields]
            image = [dg * value for value in field] + [last]
            number = 0
            for degree in range(2 * ITERS):
                sums[number] += field[degree // 2] * image[degree - degree // 2]
                number += 1
            for i in range(ITERS + 1):
                for j in range(i, ITERS + 1):
                    sums[number] += image[i] * image[j]
                    number += 1
        return tuple(sums)

    return lax.fori_loop(tiles.start, tiles.stop, body, tuple(sums))


def own_kernel(grid, rhs_ref, turned_ref, ge_ref, gs_ref, di_ref, dg_ref, v0):
    rows, cols, scen = rhs_ref.shape
    tiles = range(FIRST // TILE, FIRST // TILE + cols // TILE)
    later, below = range(tiles.start + 1, tiles.stop), range(1, rows)
    ge, gs, di, dg = conductances(grid, rows, turned_ref)
    spread(ge, ge_ref, range(rows), tiles)
    spread(gs, gs_ref, range(rows), tiles)
    spread(di, di_ref, below, later)
    spread(dg, dg_ref, below, later)
    start_own(rhs_ref, di_ref, v0, below, later)


def start_own(rhs_ref, di_ref, v0, rows, tiles, together=1):
    def body(tile):
        for row in rows:
            di = di_ref[HALO + row, tile_at(tile), :]
            for half in range(v0.shape[0]):
                value = rhs_ref[row, tile_at(tile - FIRST // TILE), half_lanes(half)]
                v0[half, HALO + row, tile_at(tile), :] = value * di

    over(tiles, body, together)


def start_side(side_a, side_b, di_ref, v0, rows, cols):
    even = is_even(COL)
    for row in rows:
        for half in range(v0.shape[0]):
            at = (row // 2, slice(row % 2 * HALO, (row % 2 + 1) * HALO), half_lanes(half))
            west, east = get(side_a, side_b, even, at)
            for piece, start in ((west, FIRST - HALO), (east, FIRST + cols)):
                where = slice(start, start + HALO)
                v0[half, HALO + row, where, :] = piece * di_ref[HALO + row, where, :]


def inner_kernel(
    grid, rhs_ref, turned_ref, side_a, side_b, *refs
):
    (ge_ref, gs_ref, di_ref, dg_ref, v0, v1, v2, v3, sums_ref) = refs[5:]
    coef, fields = (ge_ref, gs_ref, di_ref, dg_ref), (v0, v1, v2, v3)
    rows, cols, scen = rhs_ref.shape
    own = range(FIRST // TILE, FIRST // TILE + cols // TILE)
    low, high = own.start - 1, own.stop
    below = range(1, rows)
    west, east = get(side_a, side_b, is_even(COL), (rows // 2, slice(None), half_lanes(0)))
    ge, gs, di, dg = conductances(grid, rows, turned_ref, west, east)
    spread(ge, ge_ref, range(rows), (low, high))
    spread(gs, gs_ref, range(rows), (low, high))
    spread(di, di_ref, below, (low, own.start, high))
    spread(dg, dg_ref, below, (own.start,))
    start_own(rhs_ref, di_ref, v0, below, range(own.start, own.start + 1))
    start_side(side_a, side_b, di_ref, v0, below, cols)
    for level in range(1, ITERS):
        run = range(1 + level, rows - level)
        step(fields[level - 1], fields[level], coef, (run,), range(low, high + 1))
    for half in range(scen // LANES):
        sums = [jnp.zeros((TILE, LANES), jnp.float32)] * COUNT
        sums = gram(fields, coef, half, range(1 + ITERS, rows - ITERS), own, sums)
        for number, value in enumerate(sums):
            sums_ref[half, number] = value


def outer_kernel(
    grid, rhs_ref, turned_ref, side_a, side_b, end_a, end_b, inner_ref, *refs
):
    (ge_ref, gs_ref, di_ref, dg_ref, v0, v1, v2, v3, sums_ref) = refs[8:]
    coef, fields = (ge_ref, gs_ref, di_ref, dg_ref), (v0, v1, v2, v3)
    rows, cols, scen = rhs_ref.shape
    own = range(FIRST // TILE, FIRST // TILE + cols // TILE)
    reach = range(own.start - 1, own.stop + 1)
    across = cols // TILE + 1
    even_row = is_even(ROW)
    west, east = get(side_a, side_b, is_even(COL), (rows // 2, slice(None), half_lanes(0)))
    blank = jnp.zeros((TILE, LANES), jnp.float32)
    ends = [[blank], [blank]]
    for number in range(cols // TILE + 2):
        at = (HALO * across + number // 2, slice(None), half_lanes(number % 2))
        for pieces, value in zip(ends, get(end_a, end_b, even_row, at), strict=True):
            pieces.append(value)
    north, south = (jnp.concatenate(pieces + [blank], axis=0) for pieces in ends)
    above, under = range(-HALO, 0), range(rows, rows + HALO)
    ge, gs, di, dg = conductances(grid, rows, turned_ref, west, east, north, south)
    outside = (*above, *under)
    spread(ge, ge_ref, outside, reach)
    spread(gs, gs_ref, outside, reach)
    spread(di, di_ref, (*above, 0, *under), reach)
    spread(dg, dg_ref, (0,), own)
    start_own(rhs_ref, di_ref, v0, (0,), own, len(own))
    start_side(side_a, side_b, di_ref, v0, (0,), cols)
    for number in range(HALO):
        for half in range(scen // LANES):
            for tile in reach:
                block = number * across + (across - 1 if tile == reach.start else tile - own.start)
                pair = get(end_a, end_b, even_row, (block, slice(None), half_lanes(half)))
                for value, row in zip(pair, (HALO + above[number], HALO + under[number]), strict=True):
                    v0[half, row, tile_at(tile), :] = value * di_ref[row, tile_at(tile), :]
    for level in range(1, ITERS):
        runs = (range(level - HALO, level + 1), range(rows - level, rows + HALO - level))
        step(fields[level - 1], fields[level], coef, runs, reach, 3)
    for half in range(scen // LANES):
        sums = [inner_ref[half, number] for number in range(COUNT)]
        sums = gram(fields, coef, half, (*range(ITERS + 1), *range(rows - ITERS, rows)), own, sums)
        for number in range(SUMS):
            value = jnp.sum(sums[number], axis=0, keepdims=True) if number < COUNT else jnp.zeros((1, LANES))
            sums_ref[number : number + 1, half_lanes(half)] = value


def basis(grid, rhs, turned, side):
    rows, cols, scen = rhs.shape
    halves = scen // LANES
    tall, wide = rows + 2 * HALO, cols + 4 * TILE
    coef = [resident(tall, wide, LANES)] * 4
    field = resident(halves, tall, wide, LANES)
    params = pltpu.CompilerParams(vmem_limit_bytes=4 * MIB)

    def cost(microseconds):
        return pl.CostEstimate(flops=0, bytes_accessed=int(microseconds * 3.0e6), transcendentals=0)

    *coefs, v0 = pl.pallas_call(
        lambda *refs: own_kernel(grid, *refs),
        in_specs=[ON_CHIP] * 2,
        out_specs=[ON_CHIP] * 5,
        out_shape=coef + [field],
        compiler_params=params,
        cost_estimate=cost(8),
    )(rhs, turned)
    end = swaps(*messages(rhs, turned, *side, coefs[0]), ROW)
    partial = resident(halves, SUMS, TILE, LANES)
    *coefs, v0, v1, v2, v3, sums = pl.pallas_call(
        lambda *refs: inner_kernel(grid, *refs),
        in_specs=[ON_CHIP] * 9,
        out_specs=[ON_CHIP] * 9,
        out_shape=coef + [field] * ITERS + [partial],
        input_output_aliases={4 + n: n for n in range(5)},
        compiler_params=params,
        cost_estimate=cost(14),
    )(rhs, turned, *side, *coefs, v0)

    state = [*coefs, v0, v1, v2, v3]
    *out, total = pl.pallas_call(
        lambda *refs: outer_kernel(grid, *refs),
        in_specs=[ON_CHIP] * 15,
        out_specs=[ON_CHIP] * 9,
        out_shape=coef + [field] * ITERS + [resident(SUMS, scen)],
            input_output_aliases={7 + n: n for n in range(8)},
        compiler_params=params,
        cost_estimate=cost(7),
    )(rhs, turned, *side, *end, sums, *state)
    return out[4:], total


def coefficients(moment, square):
    count = ITERS + 1

    def product(left, right):
        powers = {}
        for i, a in left.items():
            for j, b in right.items():
                powers[i + j] = powers[i + j] + a * b if i + j in powers else a * b
        total = None
        for power, value in powers.items():
            term = value * moment[power]
            total = term if total is None else total + term
        return total

    def norm(resid):
        total = None
        for i in range(count):
            for j in range(i, count):
                if i in resid and j in resid:
                    term = resid[i] * resid[j] * square[i, j]
                    term = term if i == j else 2.0 * term
                    total = term if total is None else total + term
        return jnp.sqrt(jnp.maximum(total, 0.0))

    def plus(left, factor, right):
        out = dict(left)
        for i, b in right.items():
            out[i] = out[i] + factor * b if i in out else factor * b
        return out

    one = jnp.ones_like(moment[0])
    resid, direction, solution = {0: one}, {0: one}, {}
    gamma = moment[0]
    norms = [jnp.sqrt(square[0, 0])]
    for iteration in range(ITERS):
        image = dict(direction)
        for i, value in direction.items():
            image[i + 1] = image[i + 1] - value if i + 1 in image else -value
        alpha = gamma / product(direction, image)
        solution = plus(solution, alpha, direction)
        resid = plus(resid, -alpha, image)
        norms.append(norm(resid))
        if iteration + 1 < ITERS:
            gamma_new = product(resid, resid)
            direction = plus(resid, gamma_new / gamma, direction)
            gamma = gamma_new
    return [solution[i] for i in range(ITERS)], norms


def combine_kernel(sums_ref, v0, v1, v2, v3, out_hbm, norms_ref, factor_ref, buf, sem):
    scen, rows, cols = out_hbm.shape
    line = lambda n: sums_ref[n : n + 1, :]
    moment = [line(n) for n in range(2 * ITERS)]
    square, number = {}, 2 * ITERS
    for i in range(ITERS + 1):
        for j in range(i, ITERS + 1):
            square[i, j] = line(number)
            number += 1
    factors, norms = coefficients(moment, square)
    for number, value in enumerate(factors):
        factor_ref[number : number + 1, :] = value
    for number, value in enumerate(norms):
        norms_ref[number : number + 1, :] = value

    def copy(chunk):
        target = out_hbm.at[:, chunk * TILE : (chunk + 1) * TILE, :]
        return pltpu.make_async_copy(buf.at[chunk], target, sem.at[chunk])

    for chunk in range(rows // TILE):
        flat = buf.at[chunk].reshape(scen * TILE, cols)
        for inner in range(TILE):
            row = HALO + chunk * TILE + inner
            for half in range(scen // LANES):
                factor = [factor_ref[n : n + 1, half_lanes(half)] for n in range(ITERS)]
                part = [f * v[half, row, FIRST : FIRST + cols, :] for f, v in zip(factor, (v0, v1, v2, v3), strict=True)]
                value = (part[0] + part[1]) + (part[2] + part[3])
                flat[pl.ds(half * LANES * TILE + inner, LANES, stride=TILE), :] = value.T
        copy(chunk).start()
    for chunk in range(rows // TILE):
        copy(chunk).wait()


def combine(sums, fields, scen, rows, cols):
    drop, norms = pl.pallas_call(
        combine_kernel,
        in_specs=[ON_CHIP] * 5,
        out_specs=[IN_HBM, ON_CHIP],
        out_shape=[
            jax.ShapeDtypeStruct((scen, rows, cols), jnp.float32),
            jax.ShapeDtypeStruct((ITERS + 1, scen), jnp.float32),
        ],
        scratch_shapes=[
            pltpu.VMEM((TILE, scen), jnp.float32),
            pltpu.VMEM((rows // TILE, scen, TILE, cols), jnp.float32),
            pltpu.SemaphoreType.DMA((rows // TILE,)),
        ],
        compiler_params=pltpu.CompilerParams(vmem_limit_bytes=8 * MIB),
    )(sums, *fields)
    return drop, norms.T


def sum_everywhere(value):
    for axis in ("core", "z", "y", "x"):
        count = lax.axis_size(axis)
        others = [lax.ppermute(value, axis, [(i, i ^ flip) for i in range(count)]) for flip in range(1, count)]
        if count == 4:
            value = (value + others[0]) + (others[1] + others[2])
        else:
            value = value + others[0]
    return value


def local(edge_h, edge_v, pads, loads, scales):
    scen, rows, cols = loads.shape
    grid = (rows * lax.axis_size(ROW), cols * lax.axis_size(COL))
    rhs, turned, *side = prepare(loads, scales.T, edge_h, edge_v, pads)
    side = swaps(*side, COL)
    fields, sums = basis(grid, rhs, turned, side)
    return combine(sum_everywhere(sums), fields, scen, rows, cols)


def solution(mesh):
    finer = Mesh(mesh.devices.reshape(4, 2, 4, 4), ("x", "core", "y", "z"))
    in_specs = (P(ROW, COL), P(ROW, COL), P(ROW, COL), P(None, ROW, COL), P())
    out_specs = (P(None, ROW, COL), P())
    return jax.shard_map(local, mesh=finer, in_specs=in_specs, out_specs=out_specs, check_vma=False)
```

```python
import functools

import jax
import jax.numpy as jnp
from jax import lax
from jax.experimental import pallas as pl
from jax.experimental.layout import Layout, with_layout_constraint
from jax.experimental.pallas import tpu as pltpu
from jax.sharding import Mesh
from jax.sharding import PartitionSpec as P

ITERS = 4
ROW = ("x", "core")
COL = ("y", "z")

edge_table = (0.5, 0.8, 1.2, 1.7, 2.3, 3.0, 3.8, 4.7)
load_table = (0.25, 0.5, 1.0, 1.5, 2.0, 3.0, 4.0, 6.0)
pad_conductance = 20.0
leakage = 0.05

LANES = 128
TILE = 8
HALO = ITERS
FIRST = 2 * TILE
LEFT = TILE
COUNT = 2 * ITERS + (ITERS + 1) * (ITERS + 2) // 2
SUMS = 24
PRODUCT_LOSS = 4000.0
NORM_LOSS = 8000.0
MIB = 1024 * 1024
ON_CHIP = pl.BlockSpec(memory_space=pltpu.VMEM)
IN_HBM = pl.BlockSpec(memory_space=pltpu.HBM)


def resident(*shape):
    return pltpu.VMEM(shape, jnp.float32)


def lookup(classes, table):
    total = jnp.zeros(classes.shape, jnp.float32)
    for number, amount in enumerate(table):
        total = total + jnp.where(classes == number, jnp.float32(amount), jnp.float32(0.0))
    return total


def is_even(axes):
    return lax.axis_index(axes[-1]) % 2 == 0


def half_lanes(half):
    return slice(half * LANES, (half + 1) * LANES)


def put(first, second, even, index, low, high):
    first[index] = jnp.where(even, high, low)
    second[index] = jnp.where(even, low, high)


def get(first, second, even, index):
    a, b = first[index], second[index]
    return jnp.where(even, b, a), jnp.where(even, a, b)


def swaps(first, second, axes):
    count = 1
    for axis in axes:
        count *= lax.axis_size(axis)
    later = [(i, i + 1) for i in range(1, count - 1, 2)]
    return (
        lax.ppermute(first, axes, [(i, i ^ 1) for i in range(count)]),
        lax.ppermute(second, axes, later + [(b, a) for a, b in later]),
    )


def pick(table, classes):
    bit = 1
    while len(table) > 1:
        odd = (classes & bit) != 0
        table = [jnp.where(odd, table[n + 1], table[n]) for n in range(0, len(table), 2)]
        bit *= 2
    return table[0]


def prepare_kernel(
    loads_hbm, scales_hbm, eh_hbm, ev_hbm, pads_hbm, rhs_ref, turned_ref, first_ref, second_ref,
    buf, scales_ref, classes_ref, sem, small_sem,
):
    scen, rows, cols = loads_hbm.shape
    chunks = rows // TILE
    small = [pltpu.make_async_copy(scales_hbm, scales_ref, small_sem.at[3])]
    for array, source in enumerate((eh_hbm, ev_hbm, pads_hbm)):
        target = classes_ref.at[array * rows : (array + 1) * rows, :]
        small.append(pltpu.make_async_copy(source, target, small_sem.at[array]))
    for one in small:
        one.start()

    def copy(chunk):
        source = loads_hbm.at[:, chunk * TILE : (chunk + 1) * TILE, :]
        return pltpu.make_async_copy(source, buf.at[chunk], sem.at[chunk])

    for chunk in range(chunks):
        copy(chunk).start()
    even = is_even(COL)
    for one in small:
        one.wait()
    classes = classes_ref[...].astype(jnp.float32)
    classes = jnp.concatenate([classes, jnp.zeros((LANES - 3 * rows, cols), jnp.float32)], axis=0)
    turned_ref[...] = classes.T
    low, high = turned_ref[:TILE, :], turned_ref[cols - TILE :, :]
    put(first_ref, second_ref, even, (rows // 2, slice(None), half_lanes(0)), low, high)
    put(first_ref, second_ref, even, (rows // 2, slice(None), half_lanes(1)), low, high)
    weights = jnp.concatenate(
        [-scales_ref[n : n + 1, :] * jnp.float32(load_table[n]) for n in range(len(load_table))], axis=0
    )
    for chunk in range(chunks):
        copy(chunk).wait()
        flat = buf.at[chunk].reshape(scen * TILE, cols)
        for inner in range(TILE):
            row = chunk * TILE + inner
            for half in range(scen // LANES):
                index = flat[pl.ds(half * LANES * TILE + inner, LANES, stride=TILE), :]
                value = pick([weights[n : n + 1, half_lanes(half)] for n in range(8)], index.T)
                rhs_ref[row, :, half_lanes(half)] = value
                at = (row // 2, slice(row % 2 * HALO, (row % 2 + 1) * HALO), half_lanes(half))
                put(first_ref, second_ref, even, at, value[:HALO], value[cols - HALO :])


def prepare(loads, scales, edge_h, edge_v, pads):
    scen, rows, cols = loads.shape
    side = resident(rows // 2 + 1, TILE, scen)
    return pl.pallas_call(
        prepare_kernel,
        in_specs=[IN_HBM] * 5,
        out_specs=[ON_CHIP] * 4,
        out_shape=[resident(rows, cols, scen), resident(cols, LANES), side, side],
        scratch_shapes=[
            pltpu.VMEM((rows // TILE, scen, TILE, cols), jnp.int32),
            pltpu.VMEM(scales.shape, jnp.float32),
            pltpu.VMEM((3 * rows, cols), jnp.int32),
            pltpu.SemaphoreType.DMA((rows // TILE,)),
            pltpu.SemaphoreType.DMA((4,)),
        ],
        compiler_params=pltpu.CompilerParams(vmem_limit_bytes=12 * MIB),
        cost_estimate=pl.CostEstimate(flops=20_000_000, bytes_accessed=12 * MIB, transcendentals=0),
    )(*(pltpu.with_memory_space_constraint(a, pltpu.HBM) for a in (loads, scales, edge_h, edge_v, pads)))


def message_kernel(rhs_ref, turned_ref, side_a, side_b, _, first_ref, second_ref):
    rows, cols, scen = rhs_ref.shape
    across = cols // TILE + 1
    even_row, even_col = is_even(ROW), is_even(COL)

    def corner(row, lanes):
        west, east = get(side_a, side_b, even_col, (row // 2, slice(row % 2 * HALO, (row % 2 + 1) * HALO), lanes))
        return jnp.concatenate([east, west], axis=0)

    for row in range(HALO):
        blocks = slice(row * across, row * across + across - 1)
        for half in range(scen // LANES):
            lanes = half_lanes(half)
            low = rhs_ref[row, :, lanes].reshape(across - 1, TILE, LANES)
            high = rhs_ref[rows - HALO + row, :, lanes].reshape(across - 1, TILE, LANES)
            put(first_ref, second_ref, even_row, (blocks, slice(None), lanes), low, high)
            at = (row * across + across - 1, slice(None), lanes)
            put(first_ref, second_ref, even_row, at, corner(row, lanes), corner(rows - HALO + row, lanes))
    west, east = get(side_a, side_b, even_col, (rows // 2, slice(None), half_lanes(0)))
    tiles = [west] + [turned_ref[n * TILE : (n + 1) * TILE, :] for n in range(cols // TILE)] + [east]
    for number, tile in enumerate(tiles):
        at = (HALO * across + number // 2, slice(None), half_lanes(number % 2))
        first_ref[at] = tile
        second_ref[at] = tile


def messages(rhs, turned, side_a, side_b, after):
    rows, cols, scen = rhs.shape
    tiles = cols // TILE
    out = resident(HALO * (tiles + 1) + (tiles + 2) // 2, TILE, scen)
    return pl.pallas_call(
        message_kernel,
        in_specs=[ON_CHIP] * 5,
        out_specs=[ON_CHIP] * 2,
        out_shape=[out, out],
        compiler_params=pltpu.CompilerParams(vmem_limit_bytes=4 * MIB),
    )(rhs, turned, side_a, side_b, after)


def conductances(grid, rows, turned_ref, west=None, east=None, north=None, south=None):
    cols = turned_ref.shape[0]
    blank = jnp.zeros((TILE, LANES), jnp.float32)
    side = [blank if piece is None else piece for piece in (west, east)]
    own = jnp.concatenate([blank, side[0], turned_ref[...], side[1], blank], axis=0)
    shape = own.shape
    lane = lax.broadcasted_iota(jnp.int32, shape, 1)

    def classes(array):
        out = pltpu.roll(own, (LEFT - array * rows) % LANES, 1)
        if north is not None:
            above = pltpu.roll(north, (LEFT - (array + 1) * rows) % LANES, 1)
            below = pltpu.roll(south, (LEFT + rows - array * rows) % LANES, 1)
            out = jnp.where(lane < LEFT, above, jnp.where(lane < LEFT + rows, out, below))
        return out

    row_ids = lax.axis_index(ROW) * rows - LEFT + lane
    col_ids = lax.axis_index(COL) * cols - FIRST + lax.broadcasted_iota(jnp.int32, shape, 0)
    all_rows, all_cols = grid
    inside = (row_ids >= 0) & (row_ids < all_rows) & (col_ids >= 0) & (col_ids < all_cols)
    zero = jnp.zeros(shape, jnp.float32)
    g_east = jnp.where(inside & (col_ids < all_cols - 1), lookup(classes(0), edge_table), zero)
    g_south = jnp.where(inside & (row_ids < all_rows - 1), lookup(classes(1), edge_table), zero)
    g_west = pltpu.roll(g_east, 1, 0)
    g_north = pltpu.roll(g_south, 1, 1)
    diagonal = g_east + g_west + g_south + g_north + classes(2) * pad_conductance + leakage
    return g_east, g_south, 1.0 / diagonal, diagonal


def tile_at(tile):
    if isinstance(tile, int):
        return slice(tile * TILE, (tile + 1) * TILE)
    return pl.ds(pl.multiple_of(tile * TILE, TILE), TILE)


def over(tiles, body, together=1):
    if len(tiles) <= together:
        for tile in tiles:
            body(tile)
        return

    def turn(number, carry):
        for extra in range(together):
            body(tiles.start + number * together + extra)
        return carry

    lax.fori_loop(0, len(tiles) // together, turn, 0)


def spread(value, out, rows, tiles):
    for tile in tiles:
        piece = value[tile * TILE : (tile + 1) * TILE, :]
        for row in rows:
            lane = LEFT + row
            out[HALO + row, tile_at(tile), :] = jnp.broadcast_to(piece[:, lane : lane + 1], (TILE, LANES))


def step(old, new, coef, runs, tiles, together=1):
    ge_ref, gs_ref, di_ref, _ = coef
    halves = old.shape[0]

    def body(tile):
        at = tile * TILE
        here, east, west = tile_at(tile), pl.ds(at + 1, TILE), pl.ds(at - 1, TILE)
        for run in runs:
            top = HALO + run[0]
            north = [old[half, top - 1, here, :] for half in range(halves)]
            center = [old[half, top, here, :] for half in range(halves)]
            gn = gs_ref[top - 1, here, :]
            for row in range(top, top + len(run)):
                ge, gw = ge_ref[row, here, :], ge_ref[row, west, :]
                gs, di = gs_ref[row, here, :], di_ref[row, here, :]
                for half in range(halves):
                    south = old[half, row + 1, here, :]
                    total = (ge * old[half, row, east, :] + gw * old[half, row, west, :]) + (
                        gs * south + gn * north[half]
                    )
                    new[half, row, here, :] = total * di
                    north[half], center[half] = center[half], south
                gn = gs

    over(tiles, body, together)


def gram(fields, coef, half, rows, tiles, sums):
    ge_ref, gs_ref, _, dg_ref = coef
    v = fields[-1]

    def body(tile, sums):
        at = tile * TILE
        here, east, west = tile_at(tile), pl.ds(at + 1, TILE), pl.ds(at - 1, TILE)
        sums = list(sums)
        for own in rows:
            row = HALO + own
            last = (
                ge_ref[row, here, :] * v[half, row, east, :] + ge_ref[row, west, :] * v[half, row, west, :]
            ) + (gs_ref[row, here, :] * v[half, row + 1, here, :] + gs_ref[row - 1, here, :] * v[half, row - 1, here, :])
            dg = dg_ref[row, here, :]
            field = [ref[half, row, here, :] for ref in fields]
            image = [dg * value for value in field] + [last]
            number = 0
            for degree in range(2 * ITERS):
                sums[number] += field[degree // 2] * image[degree - degree // 2]
                number += 1
            for i in range(ITERS + 1):
                for j in range(i, ITERS + 1):
                    sums[number] += image[i] * image[j]
                    number += 1
        return tuple(sums)

    return lax.fori_loop(tiles.start, tiles.stop, body, tuple(sums))


def own_kernel(grid, rhs_ref, turned_ref, ge_ref, gs_ref, di_ref, dg_ref, v0):
    rows, cols, scen = rhs_ref.shape
    tiles = range(FIRST // TILE, FIRST // TILE + cols // TILE)
    later, below = range(tiles.start + 1, tiles.stop), range(1, rows)
    ge, gs, di, dg = conductances(grid, rows, turned_ref)
    spread(ge, ge_ref, range(rows), tiles)
    spread(gs, gs_ref, range(rows), tiles)
    spread(di, di_ref, below, later)
    spread(dg, dg_ref, below, later)
    start_own(rhs_ref, di_ref, v0, below, later)


def start_own(rhs_ref, di_ref, v0, rows, tiles, together=1):
    def body(tile):
        for row in rows:
            di = di_ref[HALO + row, tile_at(tile), :]
            for half in range(v0.shape[0]):
                value = rhs_ref[row, tile_at(tile - FIRST // TILE), half_lanes(half)]
                v0[half, HALO + row, tile_at(tile), :] = value * di

    over(tiles, body, together)


def start_side(side_a, side_b, di_ref, v0, rows, cols):
    even = is_even(COL)
    for row in rows:
        for half in range(v0.shape[0]):
            at = (row // 2, slice(row % 2 * HALO, (row % 2 + 1) * HALO), half_lanes(half))
            west, east = get(side_a, side_b, even, at)
            for piece, start in ((west, FIRST - HALO), (east, FIRST + cols)):
                where = slice(start, start + HALO)
                v0[half, HALO + row, where, :] = piece * di_ref[HALO + row, where, :]


def inner_kernel(
    grid, rhs_ref, turned_ref, side_a, side_b, *refs
):
    (ge_ref, gs_ref, di_ref, dg_ref, v0, v1, v2, v3, sums_ref) = refs[5:]
    coef, fields = (ge_ref, gs_ref, di_ref, dg_ref), (v0, v1, v2, v3)
    rows, cols, scen = rhs_ref.shape
    own = range(FIRST // TILE, FIRST // TILE + cols // TILE)
    low, high = own.start - 1, own.stop
    below = range(1, rows)
    west, east = get(side_a, side_b, is_even(COL), (rows // 2, slice(None), half_lanes(0)))
    ge, gs, di, dg = conductances(grid, rows, turned_ref, west, east)
    spread(ge, ge_ref, range(rows), (low, high))
    spread(gs, gs_ref, range(rows), (low, high))
    spread(di, di_ref, below, (low, own.start, high))
    spread(dg, dg_ref, below, (own.start,))
    start_own(rhs_ref, di_ref, v0, below, range(own.start, own.start + 1))
    start_side(side_a, side_b, di_ref, v0, below, cols)
    for level in range(1, ITERS):
        run = range(1 + level, rows - level)
        step(fields[level - 1], fields[level], coef, (run,), range(low, high + 1))
    for half in range(scen // LANES):
        sums = [jnp.zeros((TILE, LANES), jnp.float32)] * COUNT
        sums = gram(fields, coef, half, range(1 + ITERS, rows - ITERS), own, sums)
        for number, value in enumerate(sums):
            sums_ref[half, number] = value


def outer_kernel(
    grid, rhs_ref, turned_ref, side_a, side_b, end_a, end_b, inner_ref, *refs
):
    (ge_ref, gs_ref, di_ref, dg_ref, v0, v1, v2, v3, sums_ref) = refs[8:]
    coef, fields = (ge_ref, gs_ref, di_ref, dg_ref), (v0, v1, v2, v3)
    rows, cols, scen = rhs_ref.shape
    own = range(FIRST // TILE, FIRST // TILE + cols // TILE)
    reach = range(own.start - 1, own.stop + 1)
    across = cols // TILE + 1
    even_row = is_even(ROW)
    west, east = get(side_a, side_b, is_even(COL), (rows // 2, slice(None), half_lanes(0)))
    blank = jnp.zeros((TILE, LANES), jnp.float32)
    ends = [[blank], [blank]]
    for number in range(cols // TILE + 2):
        at = (HALO * across + number // 2, slice(None), half_lanes(number % 2))
        for pieces, value in zip(ends, get(end_a, end_b, even_row, at), strict=True):
            pieces.append(value)
    north, south = (jnp.concatenate(pieces + [blank], axis=0) for pieces in ends)
    above, under = range(-HALO, 0), range(rows, rows + HALO)
    ge, gs, di, dg = conductances(grid, rows, turned_ref, west, east, north, south)
    outside = (*above, *under)
    spread(ge, ge_ref, outside, reach)
    spread(gs, gs_ref, outside, reach)
    spread(di, di_ref, (*above, 0, *under), reach)
    spread(dg, dg_ref, (0,), own)
    start_own(rhs_ref, di_ref, v0, (0,), own, len(own))
    start_side(side_a, side_b, di_ref, v0, (0,), cols)
    for number in range(HALO):
        for half in range(scen // LANES):
            for tile in reach:
                block = number * across + (across - 1 if tile == reach.start else tile - own.start)
                pair = get(end_a, end_b, even_row, (block, slice(None), half_lanes(half)))
                for value, row in zip(pair, (HALO + above[number], HALO + under[number]), strict=True):
                    v0[half, row, tile_at(tile), :] = value * di_ref[row, tile_at(tile), :]
    for level in range(1, ITERS):
        runs = (range(level - HALO, level + 1), range(rows - level, rows + HALO - level))
        step(fields[level - 1], fields[level], coef, runs, reach, 3)
    for half in range(scen // LANES):
        sums = [inner_ref[half, number] for number in range(COUNT)]
        sums = gram(fields, coef, half, (*range(ITERS + 1), *range(rows - ITERS, rows)), own, sums)
        for number in range(SUMS):
            value = jnp.sum(sums[number], axis=0, keepdims=True) if number < COUNT else jnp.zeros((1, LANES))
            sums_ref[number : number + 1, half_lanes(half)] = value


def basis(grid, rhs, turned, side):
    rows, cols, scen = rhs.shape
    halves = scen // LANES
    tall, wide = rows + 2 * HALO, cols + 4 * TILE
    coef = [resident(tall, wide, LANES)] * 4
    field = resident(halves, tall, wide, LANES)
    params = pltpu.CompilerParams(vmem_limit_bytes=4 * MIB)

    def cost(microseconds):
        return pl.CostEstimate(flops=0, bytes_accessed=int(microseconds * 3.0e6), transcendentals=0)

    *coefs, v0 = pl.pallas_call(
        lambda *refs: own_kernel(grid, *refs),
        in_specs=[ON_CHIP] * 2,
        out_specs=[ON_CHIP] * 5,
        out_shape=coef + [field],
        compiler_params=params,
        cost_estimate=cost(8),
    )(rhs, turned)
    end = swaps(*messages(rhs, turned, *side, coefs[0]), ROW)
    partial = resident(halves, SUMS, TILE, LANES)
    *coefs, v0, v1, v2, v3, sums = pl.pallas_call(
        lambda *refs: inner_kernel(grid, *refs),
        in_specs=[ON_CHIP] * 9,
        out_specs=[ON_CHIP] * 9,
        out_shape=coef + [field] * ITERS + [partial],
        input_output_aliases={4 + n: n for n in range(5)},
        compiler_params=params,
        cost_estimate=cost(14),
    )(rhs, turned, *side, *coefs, v0)

    state = [*coefs, v0, v1, v2, v3]
    *out, total = pl.pallas_call(
        lambda *refs: outer_kernel(grid, *refs),
        in_specs=[ON_CHIP] * 15,
        out_specs=[ON_CHIP] * 9,
        out_shape=coef + [field] * ITERS + [resident(SUMS, scen)],
            input_output_aliases={7 + n: n for n in range(8)},
        compiler_params=params,
        cost_estimate=cost(7),
    )(rhs, turned, *side, *end, sums, *state)
    return out[4:], total


def coefficients(moment, square):
    count = ITERS + 1

    worst = [jnp.zeros_like(moment[0])]

    def add(terms):
        total, size = terms[0], jnp.abs(terms[0])
        for term in terms[1:]:
            total, size = total + term, size + jnp.abs(term)
        return total, size

    def product(left, right):
        powers = {}
        for i, a in left.items():
            for j, b in right.items():
                powers[i + j] = powers[i + j] + a * b if i + j in powers else a * b
        total, size = add([value * moment[power] for power, value in powers.items()])
        worst.append(jnp.where(size <= PRODUCT_LOSS * total, 0.0, 1.0))
        return total

    def norm(resid):
        terms = []
        for i in range(count):
            for j in range(i, count):
                if i in resid and j in resid:
                    term = resid[i] * resid[j] * square[i, j]
                    terms.append(term if i == j else 2.0 * term)
        total, size = add(terms)
        value = jnp.sqrt(jnp.maximum(total, 0.0))
        scale = functools.reduce(jnp.maximum, norms + [value])
        worst.append(jnp.where(size <= NORM_LOSS * scale * jnp.maximum(value, 1e-4 * jnp.sqrt(size)), 0.0, 1.0))
        return value

    def plus(left, factor, right):
        out = dict(left)
        for i, b in right.items():
            out[i] = out[i] + factor * b if i in out else factor * b
        return out

    one = jnp.ones_like(moment[0])
    resid, direction, solution = {0: one}, {0: one}, {}
    gamma = moment[0]
    norms = [jnp.sqrt(square[0, 0])]
    for iteration in range(ITERS):
        image = dict(direction)
        for i, value in direction.items():
            image[i + 1] = image[i + 1] - value if i + 1 in image else -value
        alpha = gamma / product(direction, image)
        solution = plus(solution, alpha, direction)
        resid = plus(resid, -alpha, image)
        norms.append(norm(resid))
        if iteration + 1 < ITERS:
            gamma_new = product(resid, resid)
            direction = plus(resid, gamma_new / gamma, direction)
            gamma = gamma_new
    return [solution[i] for i in range(ITERS)], norms, functools.reduce(jnp.maximum, worst)


def combine_kernel(sums_ref, v0, v1, v2, v3, out_hbm, norms_ref, doubt_ref, factor_ref, buf, sem):
    scen, rows, cols = out_hbm.shape
    line = lambda n: sums_ref[n : n + 1, :]
    moment = [line(n) for n in range(2 * ITERS)]
    square, number = {}, 2 * ITERS
    for i in range(ITERS + 1):
        for j in range(i, ITERS + 1):
            square[i, j] = line(number)
            number += 1
    factors, norms, doubt = coefficients(moment, square)
    doubt_ref[0] = jnp.max(doubt).astype(jnp.int32)
    for number, value in enumerate(factors):
        factor_ref[number : number + 1, :] = value
    for number, value in enumerate(norms):
        norms_ref[number : number + 1, :] = value

    def copy(chunk):
        target = out_hbm.at[:, chunk * TILE : (chunk + 1) * TILE, :]
        return pltpu.make_async_copy(buf.at[chunk], target, sem.at[chunk])

    for chunk in range(rows // TILE):
        flat = buf.at[chunk].reshape(scen * TILE, cols)
        for inner in range(TILE):
            row = HALO + chunk * TILE + inner
            for half in range(scen // LANES):
                factor = [factor_ref[n : n + 1, half_lanes(half)] for n in range(ITERS)]
                part = [f * v[half, row, FIRST : FIRST + cols, :] for f, v in zip(factor, (v0, v1, v2, v3), strict=True)]
                value = (part[0] + part[1]) + (part[2] + part[3])
                flat[pl.ds(half * LANES * TILE + inner, LANES, stride=TILE), :] = value.T
        copy(chunk).start()
    for chunk in range(rows // TILE):
        copy(chunk).wait()


def combine(sums, fields, scen, rows, cols):
    drop, norms, doubt = pl.pallas_call(
        combine_kernel,
        in_specs=[ON_CHIP] * 5,
        out_specs=[IN_HBM, ON_CHIP, pl.BlockSpec(memory_space=pltpu.SMEM)],
        out_shape=[
            pltpu.HBM((scen, rows, cols), jnp.float32),
            jax.ShapeDtypeStruct((ITERS + 1, scen), jnp.float32),
            jax.ShapeDtypeStruct((1,), jnp.int32),
        ],
        scratch_shapes=[
            pltpu.VMEM((TILE, scen), jnp.float32),
            pltpu.VMEM((rows // TILE, scen, TILE, cols), jnp.float32),
            pltpu.SemaphoreType.DMA((rows // TILE,)),
        ],
        compiler_params=pltpu.CompilerParams(vmem_limit_bytes=8 * MIB),
    )(sums, *fields)
    return drop, norms, doubt[0]


def sum_everywhere(value):
    for axis in ("core", "z", "y", "x"):
        count = lax.axis_size(axis)
        others = [lax.ppermute(value, axis, [(i, i ^ flip) for i in range(count)]) for flip in range(1, count)]
        if count == 4:
            value = (value + others[0]) + (others[1] + others[2])
        else:
            value = value + others[0]
    return value


def padded_2(shard, sides, width):
    edges = {}
    for axis, dim in sides:
        devices, length = (lax.axis_size(axis), shard.shape[dim])
        up = [(i, (i + 1) % devices) for i in range(devices - 1)]
        last = lax.slice_in_dim(shard, length - width, length, axis=dim)
        leading = lax.slice_in_dim(shard, 0, width, axis=dim)
        edges[dim] = (
            lax.ppermute(last, axis, up),
            lax.ppermute(leading, axis, [(b, a) for a, b in up]),
        )
    done = []
    for _, dim in sides:
        low, high = edges[dim]
        around = [(width, width) if d in done else (0, 0) for d in range(shard.ndim)]
        shard = jnp.concatenate([jnp.pad(low, around), shard, jnp.pad(high, around)], axis=dim)
        done.append(dim)
    return shard


def passed_along(value, axis, steps):
    count = lax.axis_size(axis)
    leading, last = (max(0, -steps), min(count, count - steps))
    return lax.ppermute(value, axis, [(source, source + steps) for source in range(leading, last)])


def apply_grid(field, g_east, g_west, g_south, g_north, diagonal):
    padded = padded_2(field, ((ROW, 1), (COL, 2)), 1)
    north = padded[:, :-2, 1:-1]
    south = padded[:, 2:, 1:-1]
    west = padded[:, 1:-1, :-2]
    east = padded[:, 1:-1, 2:]
    return diagonal * field - (g_east * east + g_west * west + g_south * south + g_north * north)


def inner(left, right):
    return jnp.sum(left * right, axis=(1, 2))


def recurrence(edge_h, edge_v, pads, loads, scales):
    rows, cols = pads.shape
    row_ids = lax.axis_index(ROW) * rows + lax.broadcasted_iota(jnp.int32, (rows, cols), 0)
    col_ids = lax.axis_index(COL) * cols + lax.broadcasted_iota(jnp.int32, (rows, cols), 1)
    zero = jnp.zeros((rows, cols), jnp.float32)
    g_east = jnp.where(col_ids < cols * lax.axis_size(COL) - 1, lookup(edge_h, edge_table), zero)
    g_south = jnp.where(row_ids < rows * lax.axis_size(ROW) - 1, lookup(edge_v, edge_table), zero)
    west_rim = passed_along(g_east[:, cols - 1 :], COL, 1)
    north_rim = passed_along(g_south[rows - 1 :, :], ROW, 1)
    g_west = jnp.concatenate([west_rim, g_east[:, : cols - 1]], axis=1)
    g_north = jnp.concatenate([north_rim, g_south[: rows - 1]], axis=0)
    diagonal = (
        g_east + g_west + g_south + g_north + pads.astype(jnp.float32) * pad_conductance + leakage
    )
    weights = -scales * jnp.asarray(load_table, jnp.float32)[None, :]
    right = jnp.zeros(loads.shape, jnp.float32)
    for number in range(8):
        right = right + jnp.where(
            loads == number, weights[:, number][:, None, None], jnp.float32(0.0)
        )

    def operate(field):
        return apply_grid(field, g_east, g_west, g_south, g_north, diagonal)

    def iterate(number, carry):
        solution, resid, direction, gamma, norms = carry
        image = operate(direction)
        alpha = gamma / sum_everywhere(inner(direction, image))
        solution = solution + alpha[:, None, None] * direction
        resid = resid - alpha[:, None, None] * image
        precond = resid / diagonal
        gamma_new, squares = sum_everywhere(jnp.stack([inner(resid, precond), inner(resid, resid)]))
        norms = lax.dynamic_update_slice(norms, jnp.sqrt(squares)[None], (number + 1, 0))
        direction = precond + (gamma_new / gamma)[:, None, None] * direction
        return solution, resid, direction, gamma_new, norms

    precond = right / diagonal
    gamma, squares = sum_everywhere(jnp.stack([inner(right, precond), inner(right, right)]))
    norms = jnp.zeros((ITERS + 1, squares.shape[0]), jnp.float32).at[0].set(jnp.sqrt(squares))
    carry = (jnp.zeros_like(right), right, precond, gamma, norms)
    solution, _, _, _, norms = lax.fori_loop(0, ITERS, iterate, carry)
    return solution, norms


def local(edge_h, edge_v, pads, loads, scales):
    scen, rows, cols = loads.shape
    grid = (rows * lax.axis_size(ROW), cols * lax.axis_size(COL))
    rhs, turned, *side = prepare(loads, scales.T, edge_h, edge_v, pads)
    side = swaps(*side, COL)
    fields, sums = basis(grid, rhs, turned, side)
    drop, norms, doubt = combine(sum_everywhere(sums), fields, scen, rows, cols)
    def again(drop, norms):
        drop, norms = recurrence(edge_h, edge_v, pads, loads, scales)
        return with_layout_constraint(drop, Layout((0, 1, 2))), norms

    drop, norms = lax.cond(doubt > 0, again, lambda drop, norms: (drop, norms), drop, norms)
    return drop, norms.T


def solution(mesh):
    finer = Mesh(mesh.devices.reshape(4, 2, 4, 4), ("x", "core", "y", "z"))
    in_specs = (P(ROW, COL), P(ROW, COL), P(ROW, COL), P(None, ROW, COL), P())
    out_specs = (P(None, ROW, COL), P())
    return jax.shard_map(local, mesh=finer, in_specs=in_specs, out_specs=out_specs, check_vma=False)
```

```python
import functools

import jax
import jax.numpy as jnp
from jax import lax
from jax.experimental import pallas as pl
from jax.experimental.layout import Layout, with_layout_constraint
from jax.experimental.pallas import tpu as pltpu
from jax.sharding import Mesh
from jax.sharding import PartitionSpec as P

ITERS = 4
ROW = ("x", "core")
COL = ("y", "z")

edge_table = (0.5, 0.8, 1.2, 1.7, 2.3, 3.0, 3.8, 4.7)
load_table = (0.25, 0.5, 1.0, 1.5, 2.0, 3.0, 4.0, 6.0)
pad_conductance = 20.0
leakage = 0.05

LANES = 128
TILE = 8
HALO = ITERS
FIRST = 2 * TILE
LEFT = TILE
COUNT = 2 * ITERS + (ITERS + 1) * (ITERS + 2) // 2
SUMS = 24
PRODUCT_LOSS = 4000.0
NORM_LOSS = 8000.0
MIB = 1024 * 1024
ON_CHIP = pl.BlockSpec(memory_space=pltpu.VMEM)
IN_HBM = pl.BlockSpec(memory_space=pltpu.HBM)


def resident(*shape):
    return pltpu.VMEM(shape, jnp.float32)


def lookup(classes, table):
    total = jnp.zeros(classes.shape, jnp.float32)
    for number, amount in enumerate(table):
        total = total + jnp.where(classes == number, jnp.float32(amount), jnp.float32(0.0))
    return total


def is_even(axes):
    return lax.axis_index(axes[-1]) % 2 == 0


def half_lanes(half):
    return slice(half * LANES, (half + 1) * LANES)


def put(first, second, even, index, low, high):
    first[index] = jnp.where(even, high, low)
    second[index] = jnp.where(even, low, high)


def get(first, second, even, index):
    a, b = first[index], second[index]
    return jnp.where(even, b, a), jnp.where(even, a, b)


def swaps(first, second, axes):
    count = 1
    for axis in axes:
        count *= lax.axis_size(axis)
    later = [(i, i + 1) for i in range(1, count - 1, 2)]
    return (
        lax.ppermute(first, axes, [(i, i ^ 1) for i in range(count)]),
        lax.ppermute(second, axes, later + [(b, a) for a, b in later]),
    )


def pick(table, classes):
    bit = 1
    while len(table) > 1:
        odd = (classes & bit) != 0
        table = [jnp.where(odd, table[n + 1], table[n]) for n in range(0, len(table), 2)]
        bit *= 2
    return table[0]


def prepare_kernel(
    loads_hbm, scales_hbm, eh_hbm, ev_hbm, pads_hbm, rhs_ref, turned_ref, first_ref, second_ref,
    buf, scales_ref, classes_ref, sem, small_sem,
):
    scen, rows, cols = loads_hbm.shape
    chunks = rows // TILE
    small = [pltpu.make_async_copy(scales_hbm, scales_ref, small_sem.at[3])]
    for array, source in enumerate((eh_hbm, ev_hbm, pads_hbm)):
        target = classes_ref.at[array * rows : (array + 1) * rows, :]
        small.append(pltpu.make_async_copy(source, target, small_sem.at[array]))
    for one in small:
        one.start()

    def copy(chunk):
        source = loads_hbm.at[:, chunk * TILE : (chunk + 1) * TILE, :]
        return pltpu.make_async_copy(source, buf.at[chunk], sem.at[chunk])

    for chunk in range(chunks):
        copy(chunk).start()
    even = is_even(COL)
    for one in small:
        one.wait()
    classes = classes_ref[...].astype(jnp.float32)
    classes = jnp.concatenate([classes, jnp.zeros((LANES - 3 * rows, cols), jnp.float32)], axis=0)
    turned_ref[...] = classes.T
    low, high = turned_ref[:TILE, :], turned_ref[cols - TILE :, :]
    put(first_ref, second_ref, even, (rows // 2, slice(None), half_lanes(0)), low, high)
    put(first_ref, second_ref, even, (rows // 2, slice(None), half_lanes(1)), low, high)
    weights = jnp.concatenate(
        [-scales_ref[n : n + 1, :] * jnp.float32(load_table[n]) for n in range(len(load_table))], axis=0
    )
    for chunk in range(chunks):
        copy(chunk).wait()
        flat = buf.at[chunk].reshape(scen * TILE, cols)
        for inner in range(TILE):
            row = chunk * TILE + inner
            for half in range(scen // LANES):
                index = flat[pl.ds(half * LANES * TILE + inner, LANES, stride=TILE), :]
                value = pick([weights[n : n + 1, half_lanes(half)] for n in range(8)], index.T)
                rhs_ref[row, :, half_lanes(half)] = value
                at = (row // 2, slice(row % 2 * HALO, (row % 2 + 1) * HALO), half_lanes(half))
                put(first_ref, second_ref, even, at, value[:HALO], value[cols - HALO :])


def prepare(loads, scales, edge_h, edge_v, pads):
    scen, rows, cols = loads.shape
    side = resident(rows // 2 + 1, TILE, scen)
    return pl.pallas_call(
        prepare_kernel,
        in_specs=[IN_HBM] * 5,
        out_specs=[ON_CHIP] * 4,
        out_shape=[resident(rows, cols, scen), resident(cols, LANES), side, side],
        scratch_shapes=[
            pltpu.VMEM((rows // TILE, scen, TILE, cols), jnp.int32),
            pltpu.VMEM(scales.shape, jnp.float32),
            pltpu.VMEM((3 * rows, cols), jnp.int32),
            pltpu.SemaphoreType.DMA((rows // TILE,)),
            pltpu.SemaphoreType.DMA((4,)),
        ],
        compiler_params=pltpu.CompilerParams(vmem_limit_bytes=12 * MIB),
        cost_estimate=pl.CostEstimate(flops=20_000_000, bytes_accessed=12 * MIB, transcendentals=0),
    )(*(pltpu.with_memory_space_constraint(a, pltpu.HBM) for a in (loads, scales, edge_h, edge_v, pads)))


def message_kernel(rhs_ref, turned_ref, side_a, side_b, _, first_ref, second_ref):
    rows, cols, scen = rhs_ref.shape
    across = cols // TILE + 1
    even_row, even_col = is_even(ROW), is_even(COL)

    def corner(row, lanes):
        west, east = get(side_a, side_b, even_col, (row // 2, slice(row % 2 * HALO, (row % 2 + 1) * HALO), lanes))
        return jnp.concatenate([east, west], axis=0)

    for row in range(HALO):
        blocks = slice(row * across, row * across + across - 1)
        for half in range(scen // LANES):
            lanes = half_lanes(half)
            low = rhs_ref[row, :, lanes].reshape(across - 1, TILE, LANES)
            high = rhs_ref[rows - HALO + row, :, lanes].reshape(across - 1, TILE, LANES)
            put(first_ref, second_ref, even_row, (blocks, slice(None), lanes), low, high)
            at = (row * across + across - 1, slice(None), lanes)
            put(first_ref, second_ref, even_row, at, corner(row, lanes), corner(rows - HALO + row, lanes))
    west, east = get(side_a, side_b, even_col, (rows // 2, slice(None), half_lanes(0)))
    tiles = [west] + [turned_ref[n * TILE : (n + 1) * TILE, :] for n in range(cols // TILE)] + [east]
    for number, tile in enumerate(tiles):
        at = (HALO * across + number // 2, slice(None), half_lanes(number % 2))
        first_ref[at] = tile
        second_ref[at] = tile


def messages(rhs, turned, side_a, side_b, after):
    rows, cols, scen = rhs.shape
    tiles = cols // TILE
    out = resident(HALO * (tiles + 1) + (tiles + 2) // 2, TILE, scen)
    return pl.pallas_call(
        message_kernel,
        in_specs=[ON_CHIP] * 5,
        out_specs=[ON_CHIP] * 2,
        out_shape=[out, out],
        compiler_params=pltpu.CompilerParams(vmem_limit_bytes=4 * MIB),
    )(rhs, turned, side_a, side_b, after)


def conductances(grid, rows, turned_ref, west=None, east=None, north=None, south=None):
    cols = turned_ref.shape[0]
    blank = jnp.zeros((TILE, LANES), jnp.float32)
    side = [blank if piece is None else piece for piece in (west, east)]
    own = jnp.concatenate([blank, side[0], turned_ref[...], side[1], blank], axis=0)
    shape = own.shape
    lane = lax.broadcasted_iota(jnp.int32, shape, 1)

    def classes(array):
        out = pltpu.roll(own, (LEFT - array * rows) % LANES, 1)
        if north is not None:
            above = pltpu.roll(north, (LEFT - (array + 1) * rows) % LANES, 1)
            below = pltpu.roll(south, (LEFT + rows - array * rows) % LANES, 1)
            out = jnp.where(lane < LEFT, above, jnp.where(lane < LEFT + rows, out, below))
        return out

    row_ids = lax.axis_index(ROW) * rows - LEFT + lane
    col_ids = lax.axis_index(COL) * cols - FIRST + lax.broadcasted_iota(jnp.int32, shape, 0)
    all_rows, all_cols = grid
    inside = (row_ids >= 0) & (row_ids < all_rows) & (col_ids >= 0) & (col_ids < all_cols)
    zero = jnp.zeros(shape, jnp.float32)
    g_east = jnp.where(inside & (col_ids < all_cols - 1), lookup(classes(0), edge_table), zero)
    g_south = jnp.where(inside & (row_ids < all_rows - 1), lookup(classes(1), edge_table), zero)
    g_west = pltpu.roll(g_east, 1, 0)
    g_north = pltpu.roll(g_south, 1, 1)
    diagonal = g_east + g_west + g_south + g_north + classes(2) * pad_conductance + leakage
    return g_east, g_south, 1.0 / diagonal, diagonal


def tile_at(tile):
    if isinstance(tile, int):
        return slice(tile * TILE, (tile + 1) * TILE)
    return pl.ds(pl.multiple_of(tile * TILE, TILE), TILE)


def over(tiles, body, together=1):
    if len(tiles) <= together:
        for tile in tiles:
            body(tile)
        return

    def turn(number, carry):
        for extra in range(together):
            body(tiles.start + number * together + extra)
        return carry

    lax.fori_loop(0, len(tiles) // together, turn, 0)


def spread(value, out, rows, tiles):
    for tile in tiles:
        piece = value[tile * TILE : (tile + 1) * TILE, :]
        for row in rows:
            lane = LEFT + row
            out[HALO + row, tile_at(tile), :] = jnp.broadcast_to(piece[:, lane : lane + 1], (TILE, LANES))


def step(old, new, coef, runs, tiles, together=1):
    ge_ref, gs_ref, di_ref, _ = coef
    halves = old.shape[0]

    def body(tile):
        at = tile * TILE
        here, east, west = tile_at(tile), pl.ds(at + 1, TILE), pl.ds(at - 1, TILE)
        for run in runs:
            top = HALO + run[0]
            north = [old[half, top - 1, here, :] for half in range(halves)]
            center = [old[half, top, here, :] for half in range(halves)]
            gn = gs_ref[top - 1, here, :]
            for row in range(top, top + len(run)):
                ge, gw = ge_ref[row, here, :], ge_ref[row, west, :]
                gs, di = gs_ref[row, here, :], di_ref[row, here, :]
                for half in range(halves):
                    south = old[half, row + 1, here, :]
                    total = (ge * old[half, row, east, :] + gw * old[half, row, west, :]) + (
                        gs * south + gn * north[half]
                    )
                    new[half, row, here, :] = total * di
                    north[half], center[half] = center[half], south
                gn = gs

    over(tiles, body, together)


def gram(fields, coef, half, rows, tiles, sums):
    ge_ref, gs_ref, _, dg_ref = coef
    v = fields[-1]

    def body(tile, sums):
        at = tile * TILE
        here, east, west = tile_at(tile), pl.ds(at + 1, TILE), pl.ds(at - 1, TILE)
        sums = list(sums)
        for own in rows:
            row = HALO + own
            last = (
                ge_ref[row, here, :] * v[half, row, east, :] + ge_ref[row, west, :] * v[half, row, west, :]
            ) + (gs_ref[row, here, :] * v[half, row + 1, here, :] + gs_ref[row - 1, here, :] * v[half, row - 1, here, :])
            dg = dg_ref[row, here, :]
            field = [ref[half, row, here, :] for ref in fields]
            image = [dg * value for value in field] + [last]
            number = 0
            for degree in range(2 * ITERS):
                sums[number] += field[degree // 2] * image[degree - degree // 2]
                number += 1
            for i in range(ITERS + 1):
                for j in range(i, ITERS + 1):
                    sums[number] += image[i] * image[j]
                    number += 1
        return tuple(sums)

    return lax.fori_loop(tiles.start, tiles.stop, body, tuple(sums))


def own_kernel(grid, rhs_ref, turned_ref, ge_ref, gs_ref, di_ref, dg_ref, v0):
    rows, cols, scen = rhs_ref.shape
    tiles = range(FIRST // TILE, FIRST // TILE + cols // TILE)
    later, below = range(tiles.start + 1, tiles.stop), range(1, rows)
    ge, gs, di, dg = conductances(grid, rows, turned_ref)
    spread(ge, ge_ref, range(rows), tiles)
    spread(gs, gs_ref, range(rows), tiles)
    spread(di, di_ref, below, later)
    spread(dg, dg_ref, below, later)
    start_own(rhs_ref, di_ref, v0, below, later)


def start_own(rhs_ref, di_ref, v0, rows, tiles, together=1):
    def body(tile):
        for row in rows:
            di = di_ref[HALO + row, tile_at(tile), :]
            for half in range(v0.shape[0]):
                value = rhs_ref[row, tile_at(tile - FIRST // TILE), half_lanes(half)]
                v0[half, HALO + row, tile_at(tile), :] = value * di

    over(tiles, body, together)


def start_side(side_a, side_b, di_ref, v0, rows, cols):
    even = is_even(COL)
    for row in rows:
        for half in range(v0.shape[0]):
            at = (row // 2, slice(row % 2 * HALO, (row % 2 + 1) * HALO), half_lanes(half))
            west, east = get(side_a, side_b, even, at)
            for piece, start in ((west, FIRST - HALO), (east, FIRST + cols)):
                where = slice(start, start + HALO)
                v0[half, HALO + row, where, :] = piece * di_ref[HALO + row, where, :]


def inner_kernel(
    grid, rhs_ref, turned_ref, side_a, side_b, *refs
):
    (ge_ref, gs_ref, di_ref, dg_ref, v0, v1, v2, v3, sums_ref) = refs[5:]
    coef, fields = (ge_ref, gs_ref, di_ref, dg_ref), (v0, v1, v2, v3)
    rows, cols, scen = rhs_ref.shape
    own = range(FIRST // TILE, FIRST // TILE + cols // TILE)
    low, high = own.start - 1, own.stop
    below = range(1, rows)
    west, east = get(side_a, side_b, is_even(COL), (rows // 2, slice(None), half_lanes(0)))
    ge, gs, di, dg = conductances(grid, rows, turned_ref, west, east)
    spread(ge, ge_ref, range(rows), (low, high))
    spread(gs, gs_ref, range(rows), (low, high))
    spread(di, di_ref, below, (low, own.start, high))
    spread(dg, dg_ref, below, (own.start,))
    start_own(rhs_ref, di_ref, v0, below, range(own.start, own.start + 1))
    start_side(side_a, side_b, di_ref, v0, below, cols)
    for level in range(1, ITERS):
        run = range(1 + level, rows - level)
        step(fields[level - 1], fields[level], coef, (run,), range(low, high + 1))
    for half in range(scen // LANES):
        sums = [jnp.zeros((TILE, LANES), jnp.float32)] * COUNT
        sums = gram(fields, coef, half, range(1 + ITERS, rows - ITERS), own, sums)
        for number, value in enumerate(sums):
            sums_ref[half, number] = value


def outer_kernel(
    grid, rhs_ref, turned_ref, side_a, side_b, end_a, end_b, inner_ref, *refs
):
    (ge_ref, gs_ref, di_ref, dg_ref, v0, v1, v2, v3, sums_ref) = refs[8:]
    coef, fields = (ge_ref, gs_ref, di_ref, dg_ref), (v0, v1, v2, v3)
    rows, cols, scen = rhs_ref.shape
    own = range(FIRST // TILE, FIRST // TILE + cols // TILE)
    reach = range(own.start - 1, own.stop + 1)
    across = cols // TILE + 1
    even_row = is_even(ROW)
    west, east = get(side_a, side_b, is_even(COL), (rows // 2, slice(None), half_lanes(0)))
    blank = jnp.zeros((TILE, LANES), jnp.float32)
    ends = [[blank], [blank]]
    for number in range(cols // TILE + 2):
        at = (HALO * across + number // 2, slice(None), half_lanes(number % 2))
        for pieces, value in zip(ends, get(end_a, end_b, even_row, at), strict=True):
            pieces.append(value)
    north, south = (jnp.concatenate(pieces + [blank], axis=0) for pieces in ends)
    above, under = range(-HALO, 0), range(rows, rows + HALO)
    ge, gs, di, dg = conductances(grid, rows, turned_ref, west, east, north, south)
    outside = (*above, *under)
    spread(ge, ge_ref, outside, reach)
    spread(gs, gs_ref, outside, reach)
    spread(di, di_ref, (*above, 0, *under), reach)
    spread(dg, dg_ref, (0,), own)
    start_own(rhs_ref, di_ref, v0, (0,), own, len(own))
    start_side(side_a, side_b, di_ref, v0, (0,), cols)
    for number in range(HALO):
        for half in range(scen // LANES):
            for tile in reach:
                block = number * across + (across - 1 if tile == reach.start else tile - own.start)
                pair = get(end_a, end_b, even_row, (block, slice(None), half_lanes(half)))
                for value, row in zip(pair, (HALO + above[number], HALO + under[number]), strict=True):
                    v0[half, row, tile_at(tile), :] = value * di_ref[row, tile_at(tile), :]
    for level in range(1, ITERS):
        runs = (range(level - HALO, level + 1), range(rows - level, rows + HALO - level))
        step(fields[level - 1], fields[level], coef, runs, reach, 3)
    for half in range(scen // LANES):
        sums = [inner_ref[half, number] for number in range(COUNT)]
        sums = gram(fields, coef, half, (*range(ITERS + 1), *range(rows - ITERS, rows)), own, sums)
        for number in range(SUMS):
            value = jnp.sum(sums[number], axis=0, keepdims=True) if number < COUNT else jnp.zeros((1, LANES))
            sums_ref[number : number + 1, half_lanes(half)] = value


def basis(grid, rhs, turned, side):
    rows, cols, scen = rhs.shape
    halves = scen // LANES
    tall, wide = rows + 2 * HALO, cols + 4 * TILE
    coef = [resident(tall, wide, LANES)] * 4
    field = resident(halves, tall, wide, LANES)
    params = pltpu.CompilerParams(vmem_limit_bytes=4 * MIB)

    def cost(microseconds):
        return pl.CostEstimate(flops=0, bytes_accessed=int(microseconds * 3.0e6), transcendentals=0)

    *coefs, v0 = pl.pallas_call(
        lambda *refs: own_kernel(grid, *refs),
        in_specs=[ON_CHIP] * 2,
        out_specs=[ON_CHIP] * 5,
        out_shape=coef + [field],
        compiler_params=params,
        cost_estimate=cost(8),
    )(rhs, turned)
    end = swaps(*messages(rhs, turned, *side, coefs[0]), ROW)
    partial = resident(halves, SUMS, TILE, LANES)
    *coefs, v0, v1, v2, v3, sums = pl.pallas_call(
        lambda *refs: inner_kernel(grid, *refs),
        in_specs=[ON_CHIP] * 9,
        out_specs=[ON_CHIP] * 9,
        out_shape=coef + [field] * ITERS + [partial],
        input_output_aliases={4 + n: n for n in range(5)},
        compiler_params=params,
        cost_estimate=cost(14),
    )(rhs, turned, *side, *coefs, v0)

    state = [*coefs, v0, v1, v2, v3]
    *out, total = pl.pallas_call(
        lambda *refs: outer_kernel(grid, *refs),
        in_specs=[ON_CHIP] * 15,
        out_specs=[ON_CHIP] * 9,
        out_shape=coef + [field] * ITERS + [resident(SUMS, scen)],
            input_output_aliases={7 + n: n for n in range(8)},
        compiler_params=params,
        cost_estimate=cost(7),
    )(rhs, turned, *side, *end, sums, *state)
    return out[4:], total


def coefficients(moment, square):
    count = ITERS + 1

    worst = [jnp.zeros_like(moment[0])]

    def add(terms):
        total, size = terms[0], jnp.abs(terms[0])
        for term in terms[1:]:
            total, size = total + term, size + jnp.abs(term)
        return total, size

    def product(left, right):
        powers = {}
        for i, a in left.items():
            for j, b in right.items():
                powers[i + j] = powers[i + j] + a * b if i + j in powers else a * b
        total, size = add([value * moment[power] for power, value in powers.items()])
        worst.append(jnp.where(size <= PRODUCT_LOSS * total, 0.0, 1.0))
        return total

    def norm(resid):
        terms = []
        for i in range(count):
            for j in range(i, count):
                if i in resid and j in resid:
                    term = resid[i] * resid[j] * square[i, j]
                    terms.append(term if i == j else 2.0 * term)
        total, size = add(terms)
        value = jnp.sqrt(jnp.maximum(total, 0.0))
        scale = functools.reduce(jnp.maximum, norms + [value])
        worst.append(jnp.where(size <= NORM_LOSS * scale * jnp.maximum(value, 1e-4 * jnp.sqrt(size)), 0.0, 1.0))
        return value

    def plus(left, factor, right):
        out = dict(left)
        for i, b in right.items():
            out[i] = out[i] + factor * b if i in out else factor * b
        return out

    one = jnp.ones_like(moment[0])
    resid, direction, solution = {0: one}, {0: one}, {}
    gamma = moment[0]
    norms = [jnp.sqrt(square[0, 0])]
    for iteration in range(ITERS):
        image = dict(direction)
        for i, value in direction.items():
            image[i + 1] = image[i + 1] - value if i + 1 in image else -value
        alpha = gamma / product(direction, image)
        solution = plus(solution, alpha, direction)
        resid = plus(resid, -alpha, image)
        norms.append(norm(resid))
        if iteration + 1 < ITERS:
            gamma_new = product(resid, resid)
            direction = plus(resid, gamma_new / gamma, direction)
            gamma = gamma_new
    return [solution[i] for i in range(ITERS)], norms, functools.reduce(jnp.maximum, worst)


def combine_kernel(sums_ref, v0, v1, v2, v3, out_hbm, norms_ref, doubt_ref, factor_ref, buf, sem):
    scen, rows, cols = out_hbm.shape
    line = lambda n: sums_ref[n : n + 1, :]
    moment = [line(n) for n in range(2 * ITERS)]
    square, number = {}, 2 * ITERS
    for i in range(ITERS + 1):
        for j in range(i, ITERS + 1):
            square[i, j] = line(number)
            number += 1
    factors, norms, doubt = coefficients(moment, square)
    doubt_ref[0] = jnp.max(doubt).astype(jnp.int32)
    for number, value in enumerate(factors):
        factor_ref[number : number + 1, :] = value
    for number, value in enumerate(norms):
        norms_ref[number : number + 1, :] = value

    def copy(chunk):
        target = out_hbm.at[:, chunk * TILE : (chunk + 1) * TILE, :]
        return pltpu.make_async_copy(buf.at[chunk], target, sem.at[chunk])

    for chunk in range(rows // TILE):
        flat = buf.at[chunk].reshape(scen * TILE, cols)
        for inner in range(TILE):
            row = HALO + chunk * TILE + inner
            for half in range(scen // LANES):
                factor = [factor_ref[n : n + 1, half_lanes(half)] for n in range(ITERS)]
                part = [f * v[half, row, FIRST : FIRST + cols, :] for f, v in zip(factor, (v0, v1, v2, v3), strict=True)]
                value = (part[0] + part[1]) + (part[2] + part[3])
                flat[pl.ds(half * LANES * TILE + inner, LANES, stride=TILE), :] = value.T
        copy(chunk).start()
    for chunk in range(rows // TILE):
        copy(chunk).wait()


def combine(sums, fields, scen, rows, cols):
    drop, norms, doubt = pl.pallas_call(
        combine_kernel,
        in_specs=[ON_CHIP] * 5,
        out_specs=[IN_HBM, ON_CHIP, pl.BlockSpec(memory_space=pltpu.SMEM)],
        out_shape=[
            pltpu.HBM((scen, rows, cols), jnp.float32),
            jax.ShapeDtypeStruct((ITERS + 1, scen), jnp.float32),
            jax.ShapeDtypeStruct((1,), jnp.int32),
        ],
        scratch_shapes=[
            pltpu.VMEM((TILE, scen), jnp.float32),
            pltpu.VMEM((rows // TILE, scen, TILE, cols), jnp.float32),
            pltpu.SemaphoreType.DMA((rows // TILE,)),
        ],
        compiler_params=pltpu.CompilerParams(vmem_limit_bytes=8 * MIB),
    )(sums, *fields)
    return drop, norms, doubt[0]


def sum_everywhere(value):
    for axis in ("core", "z", "y", "x"):
        count = lax.axis_size(axis)
        others = {
            flip: lax.ppermute(value, axis, [(i, i ^ flip) for i in range(count)]) for flip in range(count - 1, 0, -1)
        }
        if count == 4:
            value = (value + others[3]) + (others[2] + others[1])
        else:
            value = value + others[1]
    return value


def padded_2(shard, sides, width):
    edges = {}
    for axis, dim in sides:
        devices, length = (lax.axis_size(axis), shard.shape[dim])
        up = [(i, (i + 1) % devices) for i in range(devices - 1)]
        last = lax.slice_in_dim(shard, length - width, length, axis=dim)
        leading = lax.slice_in_dim(shard, 0, width, axis=dim)
        edges[dim] = (
            lax.ppermute(last, axis, up),
            lax.ppermute(leading, axis, [(b, a) for a, b in up]),
        )
    done = []
    for _, dim in sides:
        low, high = edges[dim]
        around = [(width, width) if d in done else (0, 0) for d in range(shard.ndim)]
        shard = jnp.concatenate([jnp.pad(low, around), shard, jnp.pad(high, around)], axis=dim)
        done.append(dim)
    return shard


def passed_along(value, axis, steps):
    count = lax.axis_size(axis)
    leading, last = (max(0, -steps), min(count, count - steps))
    return lax.ppermute(value, axis, [(source, source + steps) for source in range(leading, last)])


def apply_grid(field, g_east, g_west, g_south, g_north, diagonal):
    padded = padded_2(field, ((ROW, 1), (COL, 2)), 1)
    north = padded[:, :-2, 1:-1]
    south = padded[:, 2:, 1:-1]
    west = padded[:, 1:-1, :-2]
    east = padded[:, 1:-1, 2:]
    return diagonal * field - (g_east * east + g_west * west + g_south * south + g_north * north)


def inner(left, right):
    return jnp.sum(left * right, axis=(1, 2))


def recurrence(edge_h, edge_v, pads, loads, scales):
    rows, cols = pads.shape
    row_ids = lax.axis_index(ROW) * rows + lax.broadcasted_iota(jnp.int32, (rows, cols), 0)
    col_ids = lax.axis_index(COL) * cols + lax.broadcasted_iota(jnp.int32, (rows, cols), 1)
    zero = jnp.zeros((rows, cols), jnp.float32)
    g_east = jnp.where(col_ids < cols * lax.axis_size(COL) - 1, lookup(edge_h, edge_table), zero)
    g_south = jnp.where(row_ids < rows * lax.axis_size(ROW) - 1, lookup(edge_v, edge_table), zero)
    west_rim = passed_along(g_east[:, cols - 1 :], COL, 1)
    north_rim = passed_along(g_south[rows - 1 :, :], ROW, 1)
    g_west = jnp.concatenate([west_rim, g_east[:, : cols - 1]], axis=1)
    g_north = jnp.concatenate([north_rim, g_south[: rows - 1]], axis=0)
    diagonal = (
        g_east + g_west + g_south + g_north + pads.astype(jnp.float32) * pad_conductance + leakage
    )
    weights = -scales * jnp.asarray(load_table, jnp.float32)[None, :]
    right = jnp.zeros(loads.shape, jnp.float32)
    for number in range(8):
        right = right + jnp.where(
            loads == number, weights[:, number][:, None, None], jnp.float32(0.0)
        )

    def operate(field):
        return apply_grid(field, g_east, g_west, g_south, g_north, diagonal)

    def iterate(number, carry):
        solution, resid, direction, gamma, norms = carry
        image = operate(direction)
        alpha = gamma / sum_everywhere(inner(direction, image))
        solution = solution + alpha[:, None, None] * direction
        resid = resid - alpha[:, None, None] * image
        precond = resid / diagonal
        gamma_new, squares = sum_everywhere(jnp.stack([inner(resid, precond), inner(resid, resid)]))
        norms = lax.dynamic_update_slice(norms, jnp.sqrt(squares)[None], (number + 1, 0))
        direction = precond + (gamma_new / gamma)[:, None, None] * direction
        return solution, resid, direction, gamma_new, norms

    precond = right / diagonal
    gamma, squares = sum_everywhere(jnp.stack([inner(right, precond), inner(right, right)]))
    norms = jnp.zeros((ITERS + 1, squares.shape[0]), jnp.float32).at[0].set(jnp.sqrt(squares))
    carry = (jnp.zeros_like(right), right, precond, gamma, norms)
    solution, _, _, _, norms = lax.fori_loop(0, ITERS, iterate, carry)
    return solution, norms


def local(edge_h, edge_v, pads, loads, scales):
    scen, rows, cols = loads.shape
    grid = (rows * lax.axis_size(ROW), cols * lax.axis_size(COL))
    rhs, turned, *side = prepare(loads, scales.T, edge_h, edge_v, pads)
    side = swaps(*side, COL)
    fields, sums = basis(grid, rhs, turned, side)
    drop, norms, doubt = combine(sum_everywhere(sums), fields, scen, rows, cols)
    def again(drop, norms):
        drop, norms = recurrence(edge_h, edge_v, pads, loads, scales)
        return with_layout_constraint(drop, Layout((0, 1, 2))), norms

    drop, norms = lax.cond(doubt > 0, again, lambda drop, norms: (drop, norms), drop, norms)
    return drop, norms.T


def solution(mesh):
    finer = Mesh(mesh.devices.reshape(4, 2, 4, 4), ("x", "core", "y", "z"))
    in_specs = (P(ROW, COL), P(ROW, COL), P(ROW, COL), P(None, ROW, COL), P())
    out_specs = (P(None, ROW, COL), P())
    return jax.shard_map(local, mesh=finer, in_specs=in_specs, out_specs=out_specs, check_vma=False)
```

```python
import functools

import jax
import jax.numpy as jnp
from jax import lax
from jax.experimental import pallas as pl
from jax.experimental.layout import Layout, with_layout_constraint
from jax.experimental.pallas import tpu as pltpu
from jax.sharding import Mesh
from jax.sharding import PartitionSpec as P

ITERS = 4
ROW = ("x", "core")
COL = ("y", "z")

edge_table = (0.5, 0.8, 1.2, 1.7, 2.3, 3.0, 3.8, 4.7)
load_table = (0.25, 0.5, 1.0, 1.5, 2.0, 3.0, 4.0, 6.0)
pad_conductance = 20.0
leakage = 0.05

LANES = 128
TILE = 8
HALO = ITERS
FIRST = 2 * TILE
LEFT = TILE
COUNT = 2 * ITERS + (ITERS + 1) * (ITERS + 2) // 2
SUMS = 24
PRODUCT_LOSS = 4000.0
NORM_LOSS = 8000.0
MIB = 1024 * 1024
ON_CHIP = pl.BlockSpec(memory_space=pltpu.VMEM)
IN_HBM = pl.BlockSpec(memory_space=pltpu.HBM)


def resident(*shape):
    return pltpu.VMEM(shape, jnp.float32)


def lookup(classes, table):
    total = jnp.zeros(classes.shape, jnp.float32)
    for number, amount in enumerate(table):
        total = total + jnp.where(classes == number, jnp.float32(amount), jnp.float32(0.0))
    return total


def is_even(axes):
    return lax.axis_index(axes[-1]) % 2 == 0


def half_lanes(half):
    return slice(half * LANES, (half + 1) * LANES)


def put(first, second, even, index, low, high):
    first[index] = jnp.where(even, high, low)
    second[index] = jnp.where(even, low, high)


def get(first, second, even, index):
    a, b = first[index], second[index]
    return jnp.where(even, b, a), jnp.where(even, a, b)


def swaps(first, second, axes):
    count = 1
    for axis in axes:
        count *= lax.axis_size(axis)
    later = [(i, i + 1) for i in range(1, count - 1, 2)]
    return (
        lax.ppermute(first, axes, [(i, i ^ 1) for i in range(count)]),
        lax.ppermute(second, axes, later + [(b, a) for a, b in later]),
    )


def pick(table, classes):
    bit = 1
    while len(table) > 1:
        odd = (classes & bit) != 0
        table = [jnp.where(odd, table[n + 1], table[n]) for n in range(0, len(table), 2)]
        bit *= 2
    return table[0]


def prepare_kernel(
    loads_hbm, scales_hbm, eh_hbm, ev_hbm, pads_hbm, rhs_ref, turned_ref, first_ref, second_ref,
    buf, scales_ref, classes_ref, sem, small_sem,
):
    scen, rows, cols = loads_hbm.shape
    chunks = rows // TILE
    small = [pltpu.make_async_copy(scales_hbm, scales_ref, small_sem.at[3])]
    for array, source in enumerate((eh_hbm, ev_hbm, pads_hbm)):
        target = classes_ref.at[array * rows : (array + 1) * rows, :]
        small.append(pltpu.make_async_copy(source, target, small_sem.at[array]))
    for one in small:
        one.start()

    def copy(chunk):
        source = loads_hbm.at[:, chunk * TILE : (chunk + 1) * TILE, :]
        return pltpu.make_async_copy(source, buf.at[chunk], sem.at[chunk])

    for chunk in range(chunks):
        copy(chunk).start()
    even = is_even(COL)
    for one in small:
        one.wait()
    classes = classes_ref[...].astype(jnp.float32)
    classes = jnp.concatenate([classes, jnp.zeros((LANES - 3 * rows, cols), jnp.float32)], axis=0)
    turned_ref[...] = classes.T
    low, high = turned_ref[:TILE, :], turned_ref[cols - TILE :, :]
    put(first_ref, second_ref, even, (rows // 2, slice(None), half_lanes(0)), low, high)
    put(first_ref, second_ref, even, (rows // 2, slice(None), half_lanes(1)), low, high)
    weights = jnp.concatenate(
        [-scales_ref[n : n + 1, :] * jnp.float32(load_table[n]) for n in range(len(load_table))], axis=0
    )
    for chunk in range(chunks):
        copy(chunk).wait()
        flat = buf.at[chunk].reshape(scen * TILE, cols)
        for inner in range(TILE):
            row = chunk * TILE + inner
            for half in range(scen // LANES):
                index = flat[pl.ds(half * LANES * TILE + inner, LANES, stride=TILE), :]
                value = pick([weights[n : n + 1, half_lanes(half)] for n in range(8)], index.T)
                rhs_ref[row, :, half_lanes(half)] = value
                at = (row // 2, slice(row % 2 * HALO, (row % 2 + 1) * HALO), half_lanes(half))
                put(first_ref, second_ref, even, at, value[:HALO], value[cols - HALO :])


def prepare(loads, scales, edge_h, edge_v, pads):
    scen, rows, cols = loads.shape
    side = resident(rows // 2 + 1, TILE, scen)
    return pl.pallas_call(
        prepare_kernel,
        in_specs=[IN_HBM] * 5,
        out_specs=[ON_CHIP] * 4,
        out_shape=[resident(rows, cols, scen), resident(cols, LANES), side, side],
        scratch_shapes=[
            pltpu.VMEM((rows // TILE, scen, TILE, cols), jnp.int32),
            pltpu.VMEM(scales.shape, jnp.float32),
            pltpu.VMEM((3 * rows, cols), jnp.int32),
            pltpu.SemaphoreType.DMA((rows // TILE,)),
            pltpu.SemaphoreType.DMA((4,)),
        ],
        compiler_params=pltpu.CompilerParams(vmem_limit_bytes=12 * MIB),
        cost_estimate=pl.CostEstimate(flops=20_000_000, bytes_accessed=12 * MIB, transcendentals=0),
    )(*(pltpu.with_memory_space_constraint(a, pltpu.HBM) for a in (loads, scales, edge_h, edge_v, pads)))


def message_kernel(rhs_ref, turned_ref, side_a, side_b, _, first_ref, second_ref):
    rows, cols, scen = rhs_ref.shape
    across = cols // TILE + 1
    even_row, even_col = is_even(ROW), is_even(COL)

    def corner(row, lanes):
        west, east = get(side_a, side_b, even_col, (row // 2, slice(row % 2 * HALO, (row % 2 + 1) * HALO), lanes))
        return jnp.concatenate([east, west], axis=0)

    for row in range(HALO):
        blocks = slice(row * across, row * across + across - 1)
        for half in range(scen // LANES):
            lanes = half_lanes(half)
            low = rhs_ref[row, :, lanes].reshape(across - 1, TILE, LANES)
            high = rhs_ref[rows - HALO + row, :, lanes].reshape(across - 1, TILE, LANES)
            put(first_ref, second_ref, even_row, (blocks, slice(None), lanes), low, high)
            at = (row * across + across - 1, slice(None), lanes)
            put(first_ref, second_ref, even_row, at, corner(row, lanes), corner(rows - HALO + row, lanes))
    west, east = get(side_a, side_b, even_col, (rows // 2, slice(None), half_lanes(0)))
    tiles = [west] + [turned_ref[n * TILE : (n + 1) * TILE, :] for n in range(cols // TILE)] + [east]
    for number, tile in enumerate(tiles):
        at = (HALO * across + number // 2, slice(None), half_lanes(number % 2))
        first_ref[at] = tile
        second_ref[at] = tile


def messages(rhs, turned, side_a, side_b, after):
    rows, cols, scen = rhs.shape
    tiles = cols // TILE
    out = resident(HALO * (tiles + 1) + (tiles + 2) // 2, TILE, scen)
    return pl.pallas_call(
        message_kernel,
        in_specs=[ON_CHIP] * 5,
        out_specs=[ON_CHIP] * 2,
        out_shape=[out, out],
        compiler_params=pltpu.CompilerParams(vmem_limit_bytes=4 * MIB),
    )(rhs, turned, side_a, side_b, after)


def conductances(grid, rows, turned_ref, west=None, east=None, north=None, south=None):
    cols = turned_ref.shape[0]
    blank = jnp.zeros((TILE, LANES), jnp.float32)
    side = [blank if piece is None else piece for piece in (west, east)]
    own = jnp.concatenate([blank, side[0], turned_ref[...], side[1], blank], axis=0)
    shape = own.shape
    lane = lax.broadcasted_iota(jnp.int32, shape, 1)

    def classes(array):
        out = pltpu.roll(own, (LEFT - array * rows) % LANES, 1)
        if north is not None:
            above = pltpu.roll(north, (LEFT - (array + 1) * rows) % LANES, 1)
            below = pltpu.roll(south, (LEFT + rows - array * rows) % LANES, 1)
            out = jnp.where(lane < LEFT, above, jnp.where(lane < LEFT + rows, out, below))
        return out

    row_ids = lax.axis_index(ROW) * rows - LEFT + lane
    col_ids = lax.axis_index(COL) * cols - FIRST + lax.broadcasted_iota(jnp.int32, shape, 0)
    all_rows, all_cols = grid
    inside = (row_ids >= 0) & (row_ids < all_rows) & (col_ids >= 0) & (col_ids < all_cols)
    zero = jnp.zeros(shape, jnp.float32)
    g_east = jnp.where(inside & (col_ids < all_cols - 1), lookup(classes(0), edge_table), zero)
    g_south = jnp.where(inside & (row_ids < all_rows - 1), lookup(classes(1), edge_table), zero)
    g_west = pltpu.roll(g_east, 1, 0)
    g_north = pltpu.roll(g_south, 1, 1)
    diagonal = g_east + g_west + g_south + g_north + classes(2) * pad_conductance + leakage
    return g_east, g_south, 1.0 / diagonal, diagonal


def tile_at(tile):
    if isinstance(tile, int):
        return slice(tile * TILE, (tile + 1) * TILE)
    return pl.ds(pl.multiple_of(tile * TILE, TILE), TILE)


def over(tiles, body, together=1):
    if len(tiles) <= together:
        for tile in tiles:
            body(tile)
        return

    def turn(number, carry):
        for extra in range(together):
            body(tiles.start + number * together + extra)
        return carry

    lax.fori_loop(0, len(tiles) // together, turn, 0)


def spread(value, out, rows, tiles):
    for tile in tiles:
        piece = value[tile * TILE : (tile + 1) * TILE, :]
        for row in rows:
            lane = LEFT + row
            out[HALO + row, tile_at(tile), :] = jnp.broadcast_to(piece[:, lane : lane + 1], (TILE, LANES))


def step(old, new, coef, runs, tiles, together=1):
    ge_ref, gs_ref, di_ref, _ = coef
    halves = old.shape[0]

    def body(tile):
        at = tile * TILE
        here, east, west = tile_at(tile), pl.ds(at + 1, TILE), pl.ds(at - 1, TILE)
        for run in runs:
            top = HALO + run[0]
            north = [old[half, top - 1, here, :] for half in range(halves)]
            center = [old[half, top, here, :] for half in range(halves)]
            gn = gs_ref[top - 1, here, :]
            for row in range(top, top + len(run)):
                ge, gw = ge_ref[row, here, :], ge_ref[row, west, :]
                gs, di = gs_ref[row, here, :], di_ref[row, here, :]
                for half in range(halves):
                    south = old[half, row + 1, here, :]
                    total = (ge * old[half, row, east, :] + gw * old[half, row, west, :]) + (
                        gs * south + gn * north[half]
                    )
                    new[half, row, here, :] = total * di
                    north[half], center[half] = center[half], south
                gn = gs

    over(tiles, body, together)


def gram(fields, coef, half, rows, tiles, sums):
    ge_ref, gs_ref, _, dg_ref = coef
    v = fields[-1]

    def body(tile, sums):
        at = tile * TILE
        here, east, west = tile_at(tile), pl.ds(at + 1, TILE), pl.ds(at - 1, TILE)
        sums = list(sums)
        for own in rows:
            row = HALO + own
            last = (
                ge_ref[row, here, :] * v[half, row, east, :] + ge_ref[row, west, :] * v[half, row, west, :]
            ) + (gs_ref[row, here, :] * v[half, row + 1, here, :] + gs_ref[row - 1, here, :] * v[half, row - 1, here, :])
            dg = dg_ref[row, here, :]
            field = [ref[half, row, here, :] for ref in fields]
            image = [dg * value for value in field] + [last]
            number = 0
            for degree in range(2 * ITERS):
                sums[number] += field[degree // 2] * image[degree - degree // 2]
                number += 1
            for i in range(ITERS + 1):
                for j in range(i, ITERS + 1):
                    sums[number] += image[i] * image[j]
                    number += 1
        return tuple(sums)

    return lax.fori_loop(tiles.start, tiles.stop, body, tuple(sums))


def own_kernel(grid, rhs_ref, turned_ref, ge_ref, gs_ref, di_ref, dg_ref, v0):
    rows, cols, scen = rhs_ref.shape
    tiles = range(FIRST // TILE, FIRST // TILE + cols // TILE)
    later, below = range(tiles.start + 1, tiles.stop), range(1, rows)
    ge, gs, di, dg = conductances(grid, rows, turned_ref)
    spread(ge, ge_ref, range(rows), tiles)
    spread(gs, gs_ref, range(rows), tiles)
    spread(di, di_ref, below, later)
    spread(dg, dg_ref, below, later)
    start_own(rhs_ref, di_ref, v0, below, later)


def start_own(rhs_ref, di_ref, v0, rows, tiles, together=1):
    def body(tile):
        for row in rows:
            di = di_ref[HALO + row, tile_at(tile), :]
            for half in range(v0.shape[0]):
                value = rhs_ref[row, tile_at(tile - FIRST // TILE), half_lanes(half)]
                v0[half, HALO + row, tile_at(tile), :] = value * di

    over(tiles, body, together)


def start_side(side_a, side_b, di_ref, v0, rows, cols):
    even = is_even(COL)
    for row in rows:
        for half in range(v0.shape[0]):
            at = (row // 2, slice(row % 2 * HALO, (row % 2 + 1) * HALO), half_lanes(half))
            west, east = get(side_a, side_b, even, at)
            for piece, start in ((west, FIRST - HALO), (east, FIRST + cols)):
                where = slice(start, start + HALO)
                v0[half, HALO + row, where, :] = piece * di_ref[HALO + row, where, :]


def inner_kernel(
    grid, rhs_ref, turned_ref, side_a, side_b, *refs
):
    (ge_ref, gs_ref, di_ref, dg_ref, v0, v1, v2, v3, sums_ref) = refs[5:]
    coef, fields = (ge_ref, gs_ref, di_ref, dg_ref), (v0, v1, v2, v3)
    rows, cols, scen = rhs_ref.shape
    own = range(FIRST // TILE, FIRST // TILE + cols // TILE)
    low, high = own.start - 1, own.stop
    below = range(1, rows)
    west, east = get(side_a, side_b, is_even(COL), (rows // 2, slice(None), half_lanes(0)))
    ge, gs, di, dg = conductances(grid, rows, turned_ref, west, east)
    spread(ge, ge_ref, range(rows), (low, high))
    spread(gs, gs_ref, range(rows), (low, high))
    spread(di, di_ref, below, (low, own.start, high))
    spread(dg, dg_ref, below, (own.start,))
    start_own(rhs_ref, di_ref, v0, below, range(own.start, own.start + 1))
    start_side(side_a, side_b, di_ref, v0, below, cols)
    for level in range(1, ITERS):
        run = range(1 + level, rows - level)
        step(fields[level - 1], fields[level], coef, (run,), range(low, high + 1))
    for half in range(scen // LANES):
        sums = [jnp.zeros((TILE, LANES), jnp.float32)] * COUNT
        sums = gram(fields, coef, half, range(1 + ITERS, rows - ITERS), own, sums)
        for number, value in enumerate(sums):
            sums_ref[half, number] = value


def outer_kernel(
    grid, rhs_ref, turned_ref, side_a, side_b, end_a, end_b, inner_ref, *refs
):
    (ge_ref, gs_ref, di_ref, dg_ref, v0, v1, v2, v3, sums_ref) = refs[8:]
    coef, fields = (ge_ref, gs_ref, di_ref, dg_ref), (v0, v1, v2, v3)
    rows, cols, scen = rhs_ref.shape
    own = range(FIRST // TILE, FIRST // TILE + cols // TILE)
    reach = range(own.start - 1, own.stop + 1)
    across = cols // TILE + 1
    even_row = is_even(ROW)
    west, east = get(side_a, side_b, is_even(COL), (rows // 2, slice(None), half_lanes(0)))
    blank = jnp.zeros((TILE, LANES), jnp.float32)
    ends = [[blank], [blank]]
    for number in range(cols // TILE + 2):
        at = (HALO * across + number // 2, slice(None), half_lanes(number % 2))
        for pieces, value in zip(ends, get(end_a, end_b, even_row, at), strict=True):
            pieces.append(value)
    north, south = (jnp.concatenate(pieces + [blank], axis=0) for pieces in ends)
    above, under = range(-HALO, 0), range(rows, rows + HALO)
    ge, gs, di, dg = conductances(grid, rows, turned_ref, west, east, north, south)
    outside = (*above, *under)
    spread(ge, ge_ref, outside, reach)
    spread(gs, gs_ref, outside, reach)
    spread(di, di_ref, (*above, 0, *under), reach)
    spread(dg, dg_ref, (0,), own)
    start_own(rhs_ref, di_ref, v0, (0,), own, len(own))
    start_side(side_a, side_b, di_ref, v0, (0,), cols)
    for number in range(HALO):
        for half in range(scen // LANES):
            for tile in reach:
                block = number * across + (across - 1 if tile == reach.start else tile - own.start)
                pair = get(end_a, end_b, even_row, (block, slice(None), half_lanes(half)))
                for value, row in zip(pair, (HALO + above[number], HALO + under[number]), strict=True):
                    v0[half, row, tile_at(tile), :] = value * di_ref[row, tile_at(tile), :]
    for level in range(1, ITERS):
        runs = (range(level - HALO, level + 1), range(rows - level, rows + HALO - level))
        step(fields[level - 1], fields[level], coef, runs, reach, 6)
    for half in range(scen // LANES):
        sums = [inner_ref[half, number] for number in range(COUNT)]
        sums = gram(fields, coef, half, (*range(ITERS + 1), *range(rows - ITERS, rows)), own, sums)
        for number in range(SUMS):
            value = jnp.sum(sums[number], axis=0, keepdims=True) if number < COUNT else jnp.zeros((1, LANES))
            sums_ref[number : number + 1, half_lanes(half)] = value


def basis(grid, rhs, turned, side):
    rows, cols, scen = rhs.shape
    halves = scen // LANES
    tall, wide = rows + 2 * HALO, cols + 4 * TILE
    coef = [resident(tall, wide, LANES)] * 4
    field = resident(halves, tall, wide, LANES)
    params = pltpu.CompilerParams(vmem_limit_bytes=4 * MIB)

    def cost(microseconds):
        return pl.CostEstimate(flops=0, bytes_accessed=int(microseconds * 3.0e6), transcendentals=0)

    *coefs, v0 = pl.pallas_call(
        lambda *refs: own_kernel(grid, *refs),
        in_specs=[ON_CHIP] * 2,
        out_specs=[ON_CHIP] * 5,
        out_shape=coef + [field],
        compiler_params=params,
        cost_estimate=cost(8),
    )(rhs, turned)
    end = swaps(*messages(rhs, turned, *side, coefs[0]), ROW)
    partial = resident(halves, SUMS, TILE, LANES)
    *coefs, v0, v1, v2, v3, sums = pl.pallas_call(
        lambda *refs: inner_kernel(grid, *refs),
        in_specs=[ON_CHIP] * 9,
        out_specs=[ON_CHIP] * 9,
        out_shape=coef + [field] * ITERS + [partial],
        input_output_aliases={4 + n: n for n in range(5)},
        compiler_params=params,
        cost_estimate=cost(14),
    )(rhs, turned, *side, *coefs, v0)

    state = [*coefs, v0, v1, v2, v3]
    *out, total = pl.pallas_call(
        lambda *refs: outer_kernel(grid, *refs),
        in_specs=[ON_CHIP] * 15,
        out_specs=[ON_CHIP] * 9,
        out_shape=coef + [field] * ITERS + [resident(SUMS, scen)],
            input_output_aliases={7 + n: n for n in range(8)},
        compiler_params=params,
        cost_estimate=cost(7),
    )(rhs, turned, *side, *end, sums, *state)
    return out[4:], total


def coefficients(moment, square):
    count = ITERS + 1

    worst = [jnp.zeros_like(moment[0])]

    def add(terms):
        total, size = terms[0], jnp.abs(terms[0])
        for term in terms[1:]:
            total, size = total + term, size + jnp.abs(term)
        return total, size

    def product(left, right):
        powers = {}
        for i, a in left.items():
            for j, b in right.items():
                powers[i + j] = powers[i + j] + a * b if i + j in powers else a * b
        total, size = add([value * moment[power] for power, value in powers.items()])
        worst.append(jnp.where(size <= PRODUCT_LOSS * total, 0.0, 1.0))
        return total

    def norm(resid):
        terms = []
        for i in range(count):
            for j in range(i, count):
                if i in resid and j in resid:
                    term = resid[i] * resid[j] * square[i, j]
                    terms.append(term if i == j else 2.0 * term)
        total, size = add(terms)
        value = jnp.sqrt(jnp.maximum(total, 0.0))
        scale = functools.reduce(jnp.maximum, norms + [value])
        worst.append(jnp.where(size <= NORM_LOSS * scale * jnp.maximum(value, 1e-4 * jnp.sqrt(size)), 0.0, 1.0))
        return value

    def plus(left, factor, right):
        out = dict(left)
        for i, b in right.items():
            out[i] = out[i] + factor * b if i in out else factor * b
        return out

    one = jnp.ones_like(moment[0])
    resid, direction, solution = {0: one}, {0: one}, {}
    gamma = moment[0]
    norms = [jnp.sqrt(square[0, 0])]
    for iteration in range(ITERS):
        image = dict(direction)
        for i, value in direction.items():
            image[i + 1] = image[i + 1] - value if i + 1 in image else -value
        alpha = gamma / product(direction, image)
        solution = plus(solution, alpha, direction)
        resid = plus(resid, -alpha, image)
        norms.append(norm(resid))
        if iteration + 1 < ITERS:
            gamma_new = product(resid, resid)
            direction = plus(resid, gamma_new / gamma, direction)
            gamma = gamma_new
    return [solution[i] for i in range(ITERS)], norms, functools.reduce(jnp.maximum, worst)


def combine_kernel(sums_ref, v0, v1, v2, v3, out_hbm, norms_ref, doubt_ref, factor_ref, buf, sem):
    scen, rows, cols = out_hbm.shape
    line = lambda n: sums_ref[n : n + 1, :]
    moment = [line(n) for n in range(2 * ITERS)]
    square, number = {}, 2 * ITERS
    for i in range(ITERS + 1):
        for j in range(i, ITERS + 1):
            square[i, j] = line(number)
            number += 1
    factors, norms, doubt = coefficients(moment, square)
    doubt_ref[0] = jnp.max(doubt).astype(jnp.int32)
    for number, value in enumerate(factors):
        factor_ref[number : number + 1, :] = value
    for number, value in enumerate(norms):
        norms_ref[number : number + 1, :] = value

    def copy(chunk):
        target = out_hbm.at[:, chunk * TILE : (chunk + 1) * TILE, :]
        return pltpu.make_async_copy(buf.at[chunk], target, sem.at[chunk])

    for chunk in range(rows // TILE):
        flat = buf.at[chunk].reshape(scen * TILE, cols)
        for inner in range(TILE):
            row = HALO + chunk * TILE + inner
            for half in range(scen // LANES):
                factor = [factor_ref[n : n + 1, half_lanes(half)] for n in range(ITERS)]
                part = [f * v[half, row, FIRST : FIRST + cols, :] for f, v in zip(factor, (v0, v1, v2, v3), strict=True)]
                value = (part[0] + part[1]) + (part[2] + part[3])
                flat[pl.ds(half * LANES * TILE + inner, LANES, stride=TILE), :] = value.T
        copy(chunk).start()
    for chunk in range(rows // TILE):
        copy(chunk).wait()


def combine(sums, fields, scen, rows, cols):
    drop, norms, doubt = pl.pallas_call(
        combine_kernel,
        in_specs=[ON_CHIP] * 5,
        out_specs=[IN_HBM, ON_CHIP, pl.BlockSpec(memory_space=pltpu.SMEM)],
        out_shape=[
            pltpu.HBM((scen, rows, cols), jnp.float32),
            jax.ShapeDtypeStruct((ITERS + 1, scen), jnp.float32),
            jax.ShapeDtypeStruct((1,), jnp.int32),
        ],
        scratch_shapes=[
            pltpu.VMEM((TILE, scen), jnp.float32),
            pltpu.VMEM((rows // TILE, scen, TILE, cols), jnp.float32),
            pltpu.SemaphoreType.DMA((rows // TILE,)),
        ],
        compiler_params=pltpu.CompilerParams(vmem_limit_bytes=8 * MIB),
    )(sums, *fields)
    return drop, norms, doubt[0]


def sum_everywhere(value):
    for axis in ("core", "z", "y", "x"):
        count = lax.axis_size(axis)
        others = {
            flip: lax.ppermute(value, axis, [(i, i ^ flip) for i in range(count)]) for flip in range(count - 1, 0, -1)
        }
        if count == 4:
            value = (value + others[3]) + (others[2] + others[1])
        else:
            value = value + others[1]
    return value


def padded_2(shard, sides, width):
    edges = {}
    for axis, dim in sides:
        devices, length = (lax.axis_size(axis), shard.shape[dim])
        up = [(i, (i + 1) % devices) for i in range(devices - 1)]
        last = lax.slice_in_dim(shard, length - width, length, axis=dim)
        leading = lax.slice_in_dim(shard, 0, width, axis=dim)
        edges[dim] = (
            lax.ppermute(last, axis, up),
            lax.ppermute(leading, axis, [(b, a) for a, b in up]),
        )
    done = []
    for _, dim in sides:
        low, high = edges[dim]
        around = [(width, width) if d in done else (0, 0) for d in range(shard.ndim)]
        shard = jnp.concatenate([jnp.pad(low, around), shard, jnp.pad(high, around)], axis=dim)
        done.append(dim)
    return shard


def passed_along(value, axis, steps):
    count = lax.axis_size(axis)
    leading, last = (max(0, -steps), min(count, count - steps))
    return lax.ppermute(value, axis, [(source, source + steps) for source in range(leading, last)])


def apply_grid(field, g_east, g_west, g_south, g_north, diagonal):
    padded = padded_2(field, ((ROW, 1), (COL, 2)), 1)
    north = padded[:, :-2, 1:-1]
    south = padded[:, 2:, 1:-1]
    west = padded[:, 1:-1, :-2]
    east = padded[:, 1:-1, 2:]
    return diagonal * field - (g_east * east + g_west * west + g_south * south + g_north * north)


def inner(left, right):
    return jnp.sum(left * right, axis=(1, 2))


def recurrence(edge_h, edge_v, pads, loads, scales):
    rows, cols = pads.shape
    row_ids = lax.axis_index(ROW) * rows + lax.broadcasted_iota(jnp.int32, (rows, cols), 0)
    col_ids = lax.axis_index(COL) * cols + lax.broadcasted_iota(jnp.int32, (rows, cols), 1)
    zero = jnp.zeros((rows, cols), jnp.float32)
    g_east = jnp.where(col_ids < cols * lax.axis_size(COL) - 1, lookup(edge_h, edge_table), zero)
    g_south = jnp.where(row_ids < rows * lax.axis_size(ROW) - 1, lookup(edge_v, edge_table), zero)
    west_rim = passed_along(g_east[:, cols - 1 :], COL, 1)
    north_rim = passed_along(g_south[rows - 1 :, :], ROW, 1)
    g_west = jnp.concatenate([west_rim, g_east[:, : cols - 1]], axis=1)
    g_north = jnp.concatenate([north_rim, g_south[: rows - 1]], axis=0)
    diagonal = (
        g_east + g_west + g_south + g_north + pads.astype(jnp.float32) * pad_conductance + leakage
    )
    weights = -scales * jnp.asarray(load_table, jnp.float32)[None, :]
    right = jnp.zeros(loads.shape, jnp.float32)
    for number in range(8):
        right = right + jnp.where(
            loads == number, weights[:, number][:, None, None], jnp.float32(0.0)
        )

    def operate(field):
        return apply_grid(field, g_east, g_west, g_south, g_north, diagonal)

    def iterate(number, carry):
        solution, resid, direction, gamma, norms = carry
        image = operate(direction)
        alpha = gamma / sum_everywhere(inner(direction, image))
        solution = solution + alpha[:, None, None] * direction
        resid = resid - alpha[:, None, None] * image
        precond = resid / diagonal
        gamma_new, squares = sum_everywhere(jnp.stack([inner(resid, precond), inner(resid, resid)]))
        norms = lax.dynamic_update_slice(norms, jnp.sqrt(squares)[None], (number + 1, 0))
        direction = precond + (gamma_new / gamma)[:, None, None] * direction
        return solution, resid, direction, gamma_new, norms

    precond = right / diagonal
    gamma, squares = sum_everywhere(jnp.stack([inner(right, precond), inner(right, right)]))
    norms = jnp.zeros((ITERS + 1, squares.shape[0]), jnp.float32).at[0].set(jnp.sqrt(squares))
    carry = (jnp.zeros_like(right), right, precond, gamma, norms)
    solution, _, _, _, norms = lax.fori_loop(0, ITERS, iterate, carry)
    return solution, norms


def local(edge_h, edge_v, pads, loads, scales):
    scen, rows, cols = loads.shape
    grid = (rows * lax.axis_size(ROW), cols * lax.axis_size(COL))
    rhs, turned, *side = prepare(loads, scales.T, edge_h, edge_v, pads)
    side = swaps(*side, COL)
    fields, sums = basis(grid, rhs, turned, side)
    drop, norms, doubt = combine(sum_everywhere(sums), fields, scen, rows, cols)
    def again(drop, norms):
        drop, norms = recurrence(edge_h, edge_v, pads, loads, scales)
        return with_layout_constraint(drop, Layout((0, 1, 2))), norms

    drop, norms = lax.cond(doubt > 0, again, lambda drop, norms: (drop, norms), drop, norms)
    return drop, norms.T


def solution(mesh):
    finer = Mesh(mesh.devices.reshape(4, 2, 4, 4), ("x", "core", "y", "z"))
    in_specs = (P(ROW, COL), P(ROW, COL), P(ROW, COL), P(None, ROW, COL), P())
    out_specs = (P(None, ROW, COL), P())
    return jax.shard_map(local, mesh=finer, in_specs=in_specs, out_specs=out_specs, check_vma=False)
```
